256 devices in a mesh: tm: 8 (over y, z_lo), space: 32 (over z_hi, x, core).
Axes of the slice: x: 4, y: 4, z: 8 (z_hi: 4, z_lo: 2; z = z_hi * 2 + z_lo), core: 2. Of those that a mesh axis runs over, the one named last changes fastest.
Arguments:
- latents: float32 [256, 16, 128], P('space', 'tm'), may hold values from -16 to 16
- timestep: int32 [1], replicated, may hold values from 0 to 979
- alpha_table: float32 [1000], replicated, may hold values from 0.02 to 1, as said below
- norm_gain: float32 [2, 4096], replicated, may hold values from 0.1 to 1.9
- head_gain: float32 [4, 128], replicated, may hold values from 0.1 to 1.9
- embed_weight: bfloat16 [128, 4096], replicated, may hold values from -4 to 4
- space_project: bfloat16 [3, 4096, 4096], P(None, None, 'space'), may hold values from -0.09375 to 0.09375
- space_output: bfloat16 [4096, 4096], P('space'), may hold values from -0.375 to 0.375
- time_project: bfloat16 [3, 4096, 4096], P(None, None, 'space'), may hold values from -0.09375 to 0.09375
- time_output: bfloat16 [4096, 4096], P('space'), may hold values from -0.375 to 0.375
- noise_weight: bfloat16 [4096, 128], replicated, may hold values from -0.09375 to 0.09375
Outputs:
- predicted_noise: float32 [256, 16, 128], P('space', 'tm')
- latents_next: float32 [256, 16, 128], P('space', 'tm')
The draws below stay inside these ranges and needn't reach their ends.
Inputs may be any that keep to these rules, and one draw needn't show every extreme that they name: `alpha_table`: strictly falling from each entry to the next.
All inputs are finite; a program needn't handle non-finite values.
Results may differ from the reference program's by a relative error of at most 0.024.
Values may be sent and summed in bfloat16 or wider, within the bound.
No kernel may reach another device: no remote copies, remote signals or barrier semaphores. Data moves between devices by JAX's collectives and lax.ppermute only.
A program may use at most 64 MiB of HBM per device.

```python
import math
import jax
import jax.numpy as jnp
from jax import lax

D = 4096
HEADS = 32
HEAD_DIM = 128
CHAN = 128
STEPS = 1000
STRIDE = 20
PATCHES = 256
FRAMES = 16
INNER = 4096
N_SPACE = 32


def draw_latents(key, part):
    key = jax.random.fold_in(key, 11)
    base_key, scale_key = jax.random.split(key, 2)
    row_scale = jnp.exp(jax.random.uniform(scale_key, (PATCHES, FRAMES, 1), jnp.float32, math.log(0.4), math.log(4.0)))
    base_values = jax.random.truncated_normal(base_key, -4.0, 4.0, (PATCHES, FRAMES, CHAN), jnp.float32)
    return base_values * row_scale


def draw_embed_weight(key, part):
    key = jax.random.fold_in(key, 12)
    base_key, scale_key = jax.random.split(key, 2)
    column_scale = jnp.exp(jax.random.uniform(scale_key, (1, D), jnp.float32, math.log(0.3), math.log(3.0)))
    base_values = jax.random.truncated_normal(base_key, -4.0, 4.0, (CHAN, D), jnp.float32)
    return (base_values * column_scale / math.sqrt(CHAN)).astype(jnp.bfloat16)


def draw_alpha_table(key, part):
    key = jax.random.fold_in(key, 13)
    jitter_key, power_key = jax.random.split(key, 2)
    jitter = jax.random.uniform(jitter_key, (STEPS,), jnp.float32)
    sharpness = jnp.exp(jax.random.uniform(power_key, (), jnp.float32, math.log(0.5), math.log(3.0)))
    positions = jnp.arange(STEPS, dtype=jnp.float32)
    angle_pos = (positions + jitter) * (0.45 * math.pi / STEPS)
    cosine = jnp.cos(angle_pos)
    return 0.02 + 0.98 * jnp.power(cosine * cosine, sharpness)


def shard_levels(key, shape, cuts, least, top_value):
    factor_of, own = 1.0, jax.random.fold_in(key, 6)
    for dim, blocks in cuts:
        steps = jnp.exp(jax.random.uniform(jax.random.fold_in(own, dim), (blocks,), jnp.float32, least / len(cuts), top_value / len(cuts)))
        factor_of = factor_of * jnp.repeat(steps, shape[dim] // blocks).reshape([-1 if axis == dim else 1 for axis in range(len(shape))])
    return factor_of


def noise(key, extent, spread, limit, shards=(), held_as=jnp.bfloat16):
    drawn = spread * jax.random.normal(key, extent, jnp.float32)
    if shards:
        drawn = drawn * shard_levels(key, extent, shards, -0.22, 0.18)
    return jnp.clip(drawn, -limit, limit).astype(held_as)


def setup_inputs(seed: int = 0) -> dict:
    keys = jax.random.split(jax.random.key(seed), 12)
    latents = draw_latents(jax.random.fold_in(keys[11], 71), 0)
    timestep = jax.random.randint(keys[1], (1,), 0, STEPS - STRIDE).astype(jnp.int32)
    alpha_table = draw_alpha_table(jax.random.fold_in(keys[11], 71), 0)
    norm_gain = jnp.clip(1.0 + 0.18 * jax.random.normal(keys[3], (2, D), jnp.float32), 0.1, 1.9)
    head_gain = jnp.clip(1.0 + 0.18 * jax.random.normal(keys[4], (4, HEAD_DIM), jnp.float32), 0.1, 1.9)
    embed_weight = draw_embed_weight(jax.random.fold_in(keys[11], 71), 0)
    space_project = noise(keys[6], (3, D, INNER), D ** -0.5, 0.09375, ((2, 32),))
    space_output = noise(keys[7], (INNER, D), (INNER // 16) ** -0.5, 0.375, ((0, 32),))
    time_project = noise(keys[8], (3, D, INNER), D ** -0.5, 0.09375, ((2, 32),))
    time_output = noise(keys[9], (INNER, D), (INNER // 16) ** -0.5, 0.375, ((0, 32),))
    noise_weight = noise(keys[10], (D, CHAN), D ** -0.5, 0.09375)
    return {"latents": latents, "timestep": timestep, "alpha_table": alpha_table, "norm_gain": norm_gain, "head_gain": head_gain, "embed_weight": embed_weight, "space_project": space_project, "space_output": space_output, "time_project": time_project, "time_output": time_output, "noise_weight": noise_weight}


epsilon = 1e-06

def time_embedding(step_now, model_width):
    half_width = model_width // 2
    positions = jnp.arange(half_width, dtype=jnp.float32)
    frequency = jnp.exp(positions * (-math.log(10000.0) / half_width))
    angles = step_now.astype(jnp.float32) * frequency
    return jnp.concatenate([jnp.sin(angles), jnp.cos(angles)])

def norm_rows(values, gain_row):
    mean_square = lax.optimization_barrier(jnp.mean(values * values, axis=-1, keepdims=True))
    return values * gain_row / jnp.sqrt(mean_square + epsilon)

def head_norm(values, gain_row, head_size):
    row_count = values.shape[0]
    reshaped = values.reshape(row_count, -1, head_size)
    return norm_rows(reshaped, gain_row).reshape(row_count, -1)

def project_rows(hidden, gain_row, weights, query_gain, key_gain, head_size):
    normed = norm_rows(hidden.astype(jnp.float32), gain_row).astype(jnp.bfloat16)
    query_proj = jnp.dot(normed, weights[0], preferred_element_type=jnp.float32)
    key_proj = jnp.dot(normed, weights[1], preferred_element_type=jnp.float32)
    value_proj = jnp.dot(normed, weights[2], preferred_element_type=jnp.float32)
    query_rows = head_norm(query_proj, query_gain, head_size).astype(jnp.bfloat16)
    key_rows = head_norm(key_proj, key_gain, head_size).astype(jnp.bfloat16)
    return (query_rows, key_rows, value_proj.astype(jnp.bfloat16))

def softmax_rows(scores):
    exp_scores = jnp.exp(scores)
    return exp_scores / lax.optimization_barrier(jnp.sum(exp_scores, axis=-1, keepdims=True))

def attend_space(query_rows, key_rows, value_rows):
    head_size = query_rows.shape[-1]
    scores = jnp.einsum('pfhd,qfhd->fhpq', query_rows.astype(jnp.float32), key_rows.astype(jnp.float32)) / math.sqrt(head_size)
    weights = softmax_rows(scores).astype(jnp.bfloat16)
    return jnp.einsum('fhpq,qfhd->pfhd', weights.astype(jnp.float32), value_rows.astype(jnp.float32)).astype(jnp.bfloat16)

def attend_time(query_rows, key_rows, value_rows):
    head_size = query_rows.shape[-1]
    scores = jnp.einsum('pfhd,pghd->phfg', query_rows.astype(jnp.float32), key_rows.astype(jnp.float32)) / math.sqrt(head_size)
    weights = softmax_rows(scores).astype(jnp.bfloat16)
    return jnp.einsum('phfg,pghd->pfhd', weights.astype(jnp.float32), value_rows.astype(jnp.float32)).astype(jnp.bfloat16)

def grouped_output(attended, weights, group_count):
    row_count = attended.shape[0]
    group_width = attended.shape[1] // group_count
    pieces_in = attended.reshape(row_count, group_count, group_width).transpose(1, 0, 2)
    weight_pieces = weights.reshape(group_count, group_width, weights.shape[1])

    def add_group(running_sum, pieces):
        term = jnp.dot(pieces[0], pieces[1], preferred_element_type=jnp.float32)
        rounded = lax.optimization_barrier(term.astype(jnp.bfloat16))
        return (running_sum + rounded.astype(jnp.float32), None)
    start_sum = jnp.zeros((row_count, weights.shape[1]), jnp.float32)
    running_sum, leftover = lax.scan(add_group, start_sum, (pieces_in, weight_pieces))
    return running_sum

def reference(latents, timestep, alpha_table, norm_gain, head_gain, embed_weight, space_project, space_output, time_project, time_output, noise_weight):
    step_now = timestep[0]
    positions = jnp.arange(STEPS, dtype=jnp.int32)
    alpha_now = jnp.sum(jnp.where(positions == step_now, alpha_table, 0.0))
    alpha_next = jnp.sum(jnp.where(positions == step_now + STRIDE, alpha_table, 0.0))
    row_count = PATCHES * FRAMES
    latent_in = latents.astype(jnp.bfloat16).reshape(row_count, CHAN)
    first = (jnp.dot(latent_in, embed_weight, preferred_element_type=jnp.float32) + time_embedding(step_now, D)).astype(jnp.bfloat16)
    shape_heads = (PATCHES, FRAMES, HEADS, HEAD_DIM)
    query_rows, key_rows, value_rows = project_rows(first, norm_gain[0], space_project, head_gain[0], head_gain[1], HEAD_DIM)
    attended = attend_space(query_rows.reshape(shape_heads), key_rows.reshape(shape_heads), value_rows.reshape(shape_heads))
    spatial_out = grouped_output(attended.reshape(row_count, INNER), space_output, N_SPACE)
    second = (first.astype(jnp.float32) + spatial_out).astype(jnp.bfloat16)
    query_rows, key_rows, value_rows = project_rows(second, norm_gain[1], time_project, head_gain[2], head_gain[3], HEAD_DIM)
    attended = attend_time(query_rows.reshape(shape_heads), key_rows.reshape(shape_heads), value_rows.reshape(shape_heads))
    temporal_out = grouped_output(attended.reshape(row_count, INNER), time_output, N_SPACE)
    third = (second.astype(jnp.float32) + temporal_out).astype(jnp.bfloat16)
    predicted_noise = jnp.dot(third, noise_weight, preferred_element_type=jnp.float32)
    current = latents.reshape(row_count, CHAN)
    latents_next = jnp.sqrt(alpha_next) * (current - jnp.sqrt(1.0 - alpha_now) * predicted_noise) / jnp.sqrt(alpha_now) + jnp.sqrt(1.0 - alpha_next) * predicted_noise
    return (predicted_noise.reshape(PATCHES, FRAMES, CHAN), latents_next.reshape(PATCHES, FRAMES, CHAN))
```

```python
import math

import jax
import jax.numpy as jnp
from jax import lax
from jax.experimental import pallas as pl
from jax.experimental.pallas import tpu as pltpu
from jax.sharding import Mesh, PartitionSpec as P

STRIDE = 20
EPS = 1e-06
NX = 4
HD = 128
BF = jnp.bfloat16
F32 = jnp.float32


def shift(value, axis, step):
    size = lax.axis_size(axis)
    return lax.ppermute(value, axis, [(i, (i + step) % size) for i in range(size)])


def time_embedding(step_now, model_width):
    half_width = model_width // 2
    positions = jnp.arange(half_width, dtype=F32)
    frequency = jnp.exp(positions * (-math.log(10000.0) / half_width))
    angles = step_now.astype(F32) * frequency
    return jnp.concatenate([jnp.sin(angles), jnp.cos(angles)])


def head_norm(values, gain):
    mean_square = jnp.mean(values * values, axis=-1, keepdims=True)
    return (values * gain * lax.rsqrt(mean_square + EPS)).astype(BF)


def weigh(scores, mask=None):
    e = jnp.exp(scores * (1.0 / math.sqrt(HD)))
    if mask is not None:
        e = jnp.where(mask, e, 0.0)
    return (e / jnp.sum(e, axis=-1, keepdims=True)).astype(BF)


def dot_t(a, b):
    return lax.dot_general(a, b, (((1,), (1,)), ((), ())), preferred_element_type=F32)


def dot(a, b):
    return jnp.dot(a, b, preferred_element_type=F32)


def space_kernel(lat_ref, embed_ref, temb_ref, fold_ref, gain_ref, out_ref):
    lat = lat_ref[...]
    width = embed_ref.shape[1]
    chunk = 512
    total = jnp.zeros((lat.shape[0], 128), F32)
    for start in range(0, width, chunk):
        first = dot(lat, embed_ref[:, start : start + chunk]) + temb_ref[:, start : start + chunk]
        first = first.astype(BF).astype(F32)
        square = first * first
        for lane in range(0, chunk, 128):
            total = total + square[:, lane : lane + 128]
    mean_square = jnp.sum(total, axis=-1, keepdims=True) * (1.0 / width)
    scale = lax.rsqrt(mean_square + EPS)
    bias = fold_ref[128:129, :].astype(F32) + fold_ref[129:130, :].astype(F32)
    proj = (dot(lat, fold_ref[:128, :]) + bias) * scale
    for head in range(2):
        base = head * 3 * HD
        query = head_norm(proj[:, base : base + HD], gain_ref[0:1, :])
        key = head_norm(proj[:, base + HD : base + 2 * HD], gain_ref[1:2, :])
        value = proj[:, base + 2 * HD : base + 3 * HD].astype(BF)
        weights = weigh(dot_t(query, key))
        out_ref[:, head * HD : (head + 1) * HD] = dot(weights, value).astype(BF)
    out_ref[:, 2 * HD :] = lat


def rolled(block, step):
    if step == 0:
        return block
    parts = []
    for z in range(NX):
        for x in range(NX):
            start = (z * NX + (x - step) % NX) * 16
            parts.append(block[start : start + 16, :])
    return jnp.concatenate(parts, axis=0)


def output_kernel(core_ref, a0, a1, a2, a3, own_ref, other_ref, out_ref, lhs_own, lhs_other):
    @pl.when(pl.program_id(0) == 0)
    def _():
        core = core_ref[0]
        for step, ref in enumerate((a0, a1, a2, a3)):
            own = ref[:, pl.ds(pl.multiple_of(core * HD, HD), HD)]
            other = ref[:, pl.ds(pl.multiple_of((1 - core) * HD, HD), HD)]
            lhs_own[:, step * HD : (step + 1) * HD] = rolled(own, step)
            lhs_other[:, step * HD : (step + 1) * HD] = rolled(other, step)

    width = own_ref.shape[2]
    own = own_ref[...].reshape(NX * HD, width)
    other = other_ref[...].reshape(NX * HD, width)
    out_ref[...] = (dot(lhs_own[...], own) + dot(lhs_other[...], other)).astype(BF)


def time_kernel(
    place_ref, x0, x1, x2, x3, gain_ref, own_ref, other_ref, head_gain_ref, att_ref, fold_ref, out_ref, proj, total
):
    step = pl.program_id(0)

    @pl.when(step == 0)
    def _():
        proj[...] = jnp.zeros_like(proj)
        total[...] = jnp.zeros_like(total)

    for k, ref in enumerate((x0, x1, x2, x3)):

        @pl.when(step == k)
        def _(k=k, ref=ref):
            rows = rolled(ref[...], k).astype(F32)
            square = rows * rows
            part = total[...]
            for lane in range(0, rows.shape[1], 128):
                part = part + square[:, lane : lane + 128]
            total[...] = part
            gained = (rows * gain_ref[0]).astype(BF)
            for part_index in range(3):
                for side, w_ref in enumerate((own_ref, other_ref)):
                    col = (side * 3 + part_index) * HD
                    proj[:, col : col + HD] += dot(gained, w_ref[part_index])

    @pl.when(step == NX - 1)
    def _():
        width = NX * x0.shape[1]
        mean_square = jnp.sum(total[...], axis=-1, keepdims=True) * (1.0 / width)
        scale = lax.rsqrt(mean_square + EPS)
        count = x0.shape[0]
        row_patch = lax.broadcasted_iota(jnp.int32, (count, count), 0) >> 4
        col_patch = lax.broadcasted_iota(jnp.int32, (count, count), 1) >> 4
        mask = row_patch == col_patch
        noise = dot(att_ref[...], fold_ref[: 2 * HD, :])
        for side in range(2):
            base = side * 3 * HD
            query = head_norm(proj[:, base : base + HD] * scale, head_gain_ref[2:3, :])
            key = head_norm(proj[:, base + HD : base + 2 * HD] * scale, head_gain_ref[3:4, :])
            value = (proj[:, base + 2 * HD : base + 3 * HD] * scale).astype(BF)
            weights = weigh(dot_t(query, key), mask)
            attended = dot(weights, value).astype(BF)
            start = (2 + side) * HD
            noise = noise + dot(attended, fold_ref[start : start + HD, :])
        out_ref[...] = noise


def body(
    latents,
    timestep,
    alpha_table,
    norm_gain,
    head_gain,
    embed_weight,
    space_project,
    space_output,
    time_project,
    time_output,
    noise_weight,
):
    width = embed_weight.shape[1]
    block = width // NX
    core = lax.axis_index("c")
    place = lax.axis_index("x")
    step_now = timestep[0]
    positions = jnp.arange(alpha_table.shape[0], dtype=jnp.int32)
    alpha_now = jnp.sum(jnp.where(positions == step_now, alpha_table, 0.0))
    alpha_next = jnp.sum(jnp.where(positions == step_now + STRIDE, alpha_table, 0.0))
    temb = time_embedding(step_now, width)[None, :]

    def in_order(own, other):
        first = jnp.where(core == 0, own, other)
        second = jnp.where(core == 0, other, own)
        return jnp.stack([first, second])

    lat_bf = latents.astype(BF)
    mine = jnp.where(core == 0, lat_bf[:, 0], lat_bf[:, 1])
    theirs = jnp.where(core == 0, lat_bf[:, 1], lat_bf[:, 0])
    piece = in_order(mine, shift(theirs, "c", 1)).transpose(1, 0, 2).reshape(16, HD)
    piece = jnp.stack([piece] + [shift(piece, "x", -d) for d in range(1, NX)])
    piece = jnp.stack([piece] + [shift(piece, "zh", -d) for d in range(1, NX)])
    lat_rows = piece.reshape(16, 16, HD).transpose(1, 0, 2).reshape(256, HD)

    scaled = temb * norm_gain[0:1]
    high = scaled.astype(BF)
    low = (scaled - high.astype(F32)).astype(BF)
    lhs = jnp.concatenate(
        [(embed_weight.astype(F32) * norm_gain[0:1]).astype(BF), high, low, jnp.zeros((14, width), BF)]
    )
    fold = jnp.concatenate([dot(lhs, space_project[i]) for i in range(3)], axis=1)
    bias = fold[128:129] + fold[129:130]
    bias_high = bias.astype(BF)
    bias_low = (bias - bias_high.astype(F32)).astype(BF)
    fold = jnp.concatenate([fold[:128].astype(BF), bias_high, bias_low, jnp.zeros((14, 3 * HD), BF)])
    fold = in_order(fold, shift(fold, "c", 1)).transpose(1, 0, 2).reshape(144, 6 * HD)

    time_other = shift(time_project, "c", 1)
    pieces = [
        lax.dynamic_slice(space_output, (0, ((place - d) % NX) * block), (HD, block)) for d in range(NX)
    ]
    out_own = jnp.stack([pieces[0]] + [shift(pieces[d], "x", -d) for d in range(1, NX)])
    out_other = shift(out_own, "c", 1)
    noise_fold = jnp.concatenate(
        [dot(space_output, noise_weight).astype(BF), dot(time_output, noise_weight).astype(BF)]
    )
    noise_other = shift(noise_fold, "c", 1)
    noise_fold = jnp.concatenate(
        [in_order(noise_fold[:HD], noise_other[:HD]).reshape(2 * HD, HD), noise_fold[HD:], noise_other[HD:]]
    )

    attended = pl.pallas_call(
        space_kernel,
        out_shape=jax.ShapeDtypeStruct((256, 3 * HD), BF),
        compiler_params=pltpu.CompilerParams(vmem_limit_bytes=32 * 1024 * 1024),
        name="space_attention",
    )(lat_rows, embed_weight, temb, fold, head_gain)

    regrouped = lax.all_to_all(attended, ("y", "zl", "c"), split_axis=0, concat_axis=0, tiled=True)
    regrouped = regrouped.reshape(16, 16, 3 * HD).transpose(1, 0, 2).reshape(256, 3 * HD)
    att = regrouped[:, : 2 * HD]
    lat_block = regrouped[:64, 2 * HD :]
    att_all = [att] + [shift(att, "x", -d) for d in range(1, NX)]

    tiles = 4
    tile = block // tiles
    partial = pl.pallas_call(
        output_kernel,
        out_shape=jax.ShapeDtypeStruct((256, block), BF),
        grid_spec=pltpu.PrefetchScalarGridSpec(
            num_scalar_prefetch=1,
            grid=(tiles,),
            in_specs=[pl.BlockSpec((256, 2 * HD), lambda i, s: (0, 0))] * NX
            + [pl.BlockSpec((NX, HD, tile), lambda i, s: (0, 0, i))] * 2,
            out_specs=pl.BlockSpec((256, tile), lambda i, s: (0, i)),
            scratch_shapes=[pltpu.VMEM((256, NX * HD), BF)] * 2,
        ),
        compiler_params=pltpu.CompilerParams(vmem_limit_bytes=32 * 1024 * 1024),
        name="space_output",
    )(core.reshape(1).astype(jnp.int32), *att_all, out_own, out_other)

    own_cols = lax.dynamic_slice(embed_weight, (0, place * block), (HD, block))
    own_temb = lax.dynamic_slice(temb, (0, place * block), (1, block))
    first_block = (dot(lat_block, own_cols) + own_temb).astype(BF).astype(F32)
    spatial_out = partial[:64].astype(F32)
    for d in range(1, NX):
        spatial_out = spatial_out + shift(partial[64 * d : 64 * (d + 1)], "zh", d).astype(F32)
    second = (first_block + spatial_out).astype(BF)
    second = jnp.concatenate([second] + [shift(second, "zh", -d) for d in range(1, NX)])
    second_all = [second] + [shift(second, "x", -d) for d in range(1, NX)]

    weight_spec = pl.BlockSpec((3, block, HD), lambda i, s: (0, (s[0] + i) % NX, 0))
    partial = pl.pallas_call(
        time_kernel,
        out_shape=jax.ShapeDtypeStruct((256, HD), F32),
        grid_spec=pltpu.PrefetchScalarGridSpec(
            num_scalar_prefetch=1,
            grid=(NX,),
            in_specs=[pl.BlockSpec((256, block), lambda i, s: (0, 0))] * NX
            + [
                pl.BlockSpec((1, 1, block), lambda i, s: ((s[0] + i) % NX, 0, 0)),
                weight_spec,
                weight_spec,
                pl.BlockSpec((4, HD), lambda i, s: (0, 0)),
                pl.BlockSpec((256, 2 * HD), lambda i, s: (0, 0)),
                pl.BlockSpec((4 * HD, HD), lambda i, s: (0, 0)),
            ],
            out_specs=pl.BlockSpec((256, HD), lambda i, s: (0, 0)),
            scratch_shapes=[pltpu.VMEM((256, 6 * HD), F32), pltpu.VMEM((256, HD), F32)],
        ),
        compiler_params=pltpu.CompilerParams(vmem_limit_bytes=40 * 1024 * 1024),
        name="time_attention",
    )(
        place.reshape(1).astype(jnp.int32),
        *second_all,
        norm_gain[1].reshape(NX, 1, block),
        time_project,
        time_other,
        head_gain,
        att,
        noise_fold,
    )

    noise = partial[:64]
    for d in range(1, NX):
        noise = noise + shift(partial[64 * d : 64 * (d + 1)], "zh", d)
    total = noise[:16]
    for d in range(1, NX):
        total = total + shift(noise[16 * d : 16 * (d + 1)], "x", d)
    total = lax.all_to_all(total, ("y", "zl"), split_axis=0, concat_axis=0, tiled=True)

    own_first = (dot(lat_bf.reshape(16, HD), embed_weight) + temb).astype(BF)
    predicted_noise = (total + dot(own_first, noise_weight)).reshape(latents.shape)
    latents_next = (
        jnp.sqrt(alpha_next)
        * (latents - jnp.sqrt(1.0 - alpha_now) * predicted_noise)
        / jnp.sqrt(alpha_now)
        + jnp.sqrt(1.0 - alpha_next) * predicted_noise
    )
    return (predicted_noise, latents_next)


def solution(mesh):
    fine = Mesh(mesh.devices.reshape(4, 2, 4, 4, 2), ("y", "zl", "zh", "x", "c"))
    space = ("zh", "x", "c")
    rows = P(space, ("y", "zl"), None)
    placed = (
        rows,
        P(),
        P(),
        P(),
        P(),
        P(),
        P(None, None, space),
        P(space, None),
        P(None, None, space),
        P(space, None),
        P(),
    )
    return jax.shard_map(
        body,
        mesh=fine,
        in_specs=placed,
        out_specs=(rows, rows),
        check_vma=False,
    )
```

```python
import math

import jax
import jax.numpy as jnp
from jax import lax
from jax.experimental import pallas as pl
from jax.experimental.pallas import tpu as pltpu
from jax.sharding import Mesh, PartitionSpec as P

STRIDE = 20
EPS = 1e-06
NX = 4
HD = 128
ORDER = (1, 3, 2)
BF = jnp.bfloat16
F32 = jnp.float32


def shift(value, axis, step):
    size = lax.axis_size(axis)
    return lax.ppermute(value, axis, [(i, (i + step) % size) for i in range(size)])


def time_embedding(step_now, model_width):
    half_width = model_width // 2
    positions = jnp.arange(half_width, dtype=F32)
    frequency = jnp.exp(positions * (-math.log(10000.0) / half_width))
    angles = step_now.astype(F32) * frequency
    return jnp.concatenate([jnp.sin(angles), jnp.cos(angles)])


def head_norm(values, gain):
    mean_square = jnp.mean(values * values, axis=-1, keepdims=True)
    return (values * gain * lax.rsqrt(mean_square + EPS)).astype(BF)


def weigh(scores, mask=None):
    e = jnp.exp(scores * (1.0 / math.sqrt(HD)))
    if mask is not None:
        e = jnp.where(mask, e, 0.0)
    return (e / jnp.sum(e, axis=-1, keepdims=True)).astype(BF)


def dot_t(a, b):
    return lax.dot_general(a, b, (((1,), (1,)), ((), ())), preferred_element_type=F32)


def dot(a, b):
    return jnp.dot(a, b, preferred_element_type=F32)


def reorder(count, source):
    row = lax.broadcasted_iota(jnp.int32, (count, count), 0)
    col = lax.broadcasted_iota(jnp.int32, (count, count), 1)
    return (col == source(row)).astype(BF)


def space_kernel(place_ref, lat_ref, embed_ref, temb_ref, fold_ref, gain_ref, out_ref):
    z_here = place_ref[1]

    def source(row):
        z = (z_here + (row >> 2)) & 3
        return (((z * 4 + (row & 3)) * 2 + ((row >> 4) & 1)) << 3) + (row >> 5)

    lat = dot(reorder(256, source), lat_ref[...]).astype(BF)
    width = embed_ref.shape[1]
    chunk = 512
    total = jnp.zeros((lat.shape[0], 128), F32)
    for start in range(0, width, chunk):
        first = dot(lat, embed_ref[:, start : start + chunk]) + temb_ref[:, start : start + chunk]
        first = first.astype(BF).astype(F32)
        square = first * first
        for lane in range(0, chunk, 128):
            total = total + square[:, lane : lane + 128]
    mean_square = jnp.sum(total, axis=-1, keepdims=True) * (1.0 / width)
    scale = lax.rsqrt(mean_square + EPS)
    bias = fold_ref[128:129, :].astype(F32) + fold_ref[129:130, :].astype(F32)
    proj = (dot(lat, fold_ref[:128, :]) + bias) * scale
    parts = []
    for head in range(2):
        base = head * 3 * HD
        query = head_norm(proj[:, base : base + HD], gain_ref[0:1, :])
        key = head_norm(proj[:, base + HD : base + 2 * HD], gain_ref[1:2, :])
        value = proj[:, base + 2 * HD : base + 3 * HD].astype(BF)
        weights = weigh(dot_t(query, key))
        parts.append(dot(weights, value).astype(BF))
    result = jnp.concatenate(parts + [lat], axis=1)
    for tm in range(8):
        for x in range(NX):
            start = (tm * NX + x) * 32
            out_ref[start : start + 32, :] = result[tm * 32 : (tm + 1) * 32, :]


def output_kernel(
    place_ref, att_ref, embed_ref, temb_ref, own_ref, other_ref, out_ref, base_ref, att_own_ref, lhs_own, lhs_other, lat
):
    @pl.when(pl.program_id(0) == 0)
    def _():
        x_here = place_ref[0]
        core = place_ref[2]
        swap = reorder(256, lambda row: ((row & 15) << 4) + (row >> 4))
        for x in range(NX):
            rows = jnp.concatenate(
                [att_ref[(tm * NX + x) * 32 : (tm * NX + x + 1) * 32, :] for tm in range(8)], axis=0
            )
            rows = dot(swap, rows).astype(BF)
            slot = pl.multiple_of(((x - x_here) & 3) * HD, HD)
            first = rows[:, :HD]
            second = rows[:, HD : 2 * HD]
            lhs_own[:, pl.ds(slot, HD)] = jnp.where(core == 0, first, second)
            lhs_other[:, pl.ds(slot, HD)] = jnp.where(core == 0, second, first)

            @pl.when(x == x_here)
            def _():
                att_own_ref[...] = rows[:, : 2 * HD]

            if x == 0:
                lat[...] = rows[:64, 2 * HD :]

    width = own_ref.shape[2]
    own = own_ref[...].reshape(NX * HD, width)
    other = other_ref[...].reshape(NX * HD, width)
    share = (dot(lhs_own[...], own) + dot(lhs_other[...], other)).astype(BF)
    out_ref[...] = share[64:, :]
    first = (dot(lat[...], embed_ref[...]) + temb_ref[...]).astype(BF)
    base_ref[...] = first.astype(F32) + share[:64, :].astype(F32)


def time_kernel(
    place_ref, x0, x1, x2, x3, gain_ref, own_ref, other_ref, head_gain_ref, att_ref, fold_ref, out_ref, proj, total
):
    step = pl.program_id(0)

    @pl.when(step == 0)
    def _():
        proj[...] = jnp.zeros_like(proj)
        total[...] = jnp.zeros_like(total)

    for k, ref in enumerate((x0, x1, x2, x3)):

        @pl.when(step == k)
        def _(ref=ref):
            rows = ref[...].astype(F32)
            square = rows * rows
            part = total[...]
            for lane in range(0, rows.shape[1], 128):
                part = part + square[:, lane : lane + 128]
            total[...] = part
            gained = (rows * gain_ref[0]).astype(BF)
            for index in range(3):
                pair = jnp.concatenate([own_ref[index], other_ref[index]], axis=1)
                proj[:, index * 2 * HD : (index + 1) * 2 * HD] += dot(gained, pair)

    @pl.when(step == NX - 1)
    def _():
        z_here = place_ref[1]
        width = NX * x0.shape[1]
        mean_square = jnp.sum(total[...], axis=-1, keepdims=True) * (1.0 / width)
        scale = lax.rsqrt(mean_square + EPS)
        count = x0.shape[0]
        row_patch = lax.broadcasted_iota(jnp.int32, (count, count), 0) >> 4
        col_patch = lax.broadcasted_iota(jnp.int32, (count, count), 1) >> 4
        mask = row_patch == col_patch
        parts = [att_ref[...]]
        for side in range(2):
            query, key, value = [
                proj[:, (2 * index + side) * HD : (2 * index + side + 1) * HD] * scale for index in range(3)
            ]
            query = head_norm(query, head_gain_ref[2:3, :])
            key = head_norm(key, head_gain_ref[3:4, :])
            weights = weigh(dot_t(query, key), mask)
            parts.append(dot(weights, value.astype(BF)).astype(BF))

        def source(row):
            z = (((row >> 3) & 3) - z_here) & 3
            return (z << 6) + (((row >> 1) & 3) << 4) + ((row >> 5) << 1) + (row & 1)

        both = dot(reorder(count, source), jnp.concatenate(parts, axis=1)).astype(BF)
        out_ref[...] = dot(both, fold_ref[...])


def body(
    latents,
    timestep,
    alpha_table,
    norm_gain,
    head_gain,
    embed_weight,
    space_project,
    space_output,
    time_project,
    time_output,
    noise_weight,
):
    width = embed_weight.shape[1]
    block = width // NX
    core = lax.axis_index("c")
    place = lax.axis_index("x")
    places = jnp.stack([place, lax.axis_index("zh"), core]).astype(jnp.int32)
    step_now = timestep[0]
    positions = jnp.arange(alpha_table.shape[0], dtype=jnp.int32)
    alpha_now = jnp.sum(jnp.where(positions == step_now, alpha_table, 0.0))
    alpha_next = jnp.sum(jnp.where(positions == step_now + STRIDE, alpha_table, 0.0))
    temb = time_embedding(step_now, width)[None, :]

    def in_order(own, other):
        first = jnp.where(core == 0, own, other)
        second = jnp.where(core == 0, other, own)
        return jnp.stack([first, second])

    lat_bf = latents.astype(BF)
    lat_rows = jnp.broadcast_to(lat_bf.transpose(1, 0, 2)[None], (16, 2, 8, HD)).reshape(256, HD)
    lat_rows = lax.all_to_all(lat_rows, ("zh", "x", "c"), split_axis=0, concat_axis=0, tiled=True)

    scaled = temb * norm_gain[0:1]
    high = scaled.astype(BF)
    low = (scaled - high.astype(F32)).astype(BF)
    lhs = jnp.concatenate(
        [(embed_weight.astype(F32) * norm_gain[0:1]).astype(BF), high, low, jnp.zeros((14, width), BF)]
    )
    fold = jnp.concatenate([dot(lhs, space_project[i]) for i in range(3)], axis=1)
    bias = fold[128:129] + fold[129:130]
    bias_high = bias.astype(BF)
    bias_low = (bias - bias_high.astype(F32)).astype(BF)
    fold = jnp.concatenate([fold[:128].astype(BF), bias_high, bias_low, jnp.zeros((14, 3 * HD), BF)])
    fold = in_order(fold, shift(fold, "c", 1)).transpose(1, 0, 2).reshape(144, 6 * HD)

    time_other = shift(time_project, "c", 1)
    pieces = [
        lax.dynamic_slice(space_output, (0, ((place - d) % NX) * block), (HD, block)) for d in range(NX)
    ]
    got = {d: shift(pieces[d], "x", -d) for d in ORDER}
    out_own = jnp.stack([pieces[0]] + [got[d] for d in range(1, NX)])
    out_other = shift(out_own, "c", 1)
    noise_fold = jnp.concatenate(
        [dot(space_output, noise_weight).astype(BF), dot(time_output, noise_weight).astype(BF)]
    )
    noise_other = shift(noise_fold, "c", 1)
    noise_fold = jnp.concatenate(
        [in_order(noise_fold[:HD], noise_other[:HD]).reshape(2 * HD, HD), noise_fold[HD:], noise_other[HD:]]
    )

    def whole(*shape):
        return pl.BlockSpec(shape, lambda i, s: (0,) * len(shape))

    attended = pl.pallas_call(
        space_kernel,
        out_shape=jax.ShapeDtypeStruct((1024, 3 * HD), BF),
        grid_spec=pltpu.PrefetchScalarGridSpec(
            num_scalar_prefetch=1,
            grid=(1,),
            in_specs=[whole(256, HD), whole(HD, width), whole(1, width), whole(144, 6 * HD), whole(4, HD)],
            out_specs=whole(1024, 3 * HD),
        ),
        compiler_params=pltpu.CompilerParams(vmem_limit_bytes=32 * 1024 * 1024),
        name="space_attention",
    )(places, lat_rows, embed_weight, temb, fold, head_gain)

    regrouped = lax.all_to_all(attended, ("y", "zl", "x", "c"), split_axis=0, concat_axis=0, tiled=True)

    tiles = 4
    tile = block // tiles
    share, base, att_own = pl.pallas_call(
        output_kernel,
        out_shape=(
            jax.ShapeDtypeStruct((192, block), BF),
            jax.ShapeDtypeStruct((64, block), F32),
            jax.ShapeDtypeStruct((256, 2 * HD), BF),
        ),
        grid_spec=pltpu.PrefetchScalarGridSpec(
            num_scalar_prefetch=1,
            grid=(tiles,),
            in_specs=[
                whole(1024, 3 * HD),
                pl.BlockSpec((HD, tile), lambda i, s: (0, s[0] * tiles + i)),
                pl.BlockSpec((1, tile), lambda i, s: (0, s[0] * tiles + i)),
                pl.BlockSpec((NX, HD, tile), lambda i, s: (0, 0, i)),
                pl.BlockSpec((NX, HD, tile), lambda i, s: (0, 0, i)),
            ],
            out_specs=[
                pl.BlockSpec((192, tile), lambda i, s: (0, i)),
                pl.BlockSpec((64, tile), lambda i, s: (0, i)),
                whole(256, 2 * HD),
            ],
            scratch_shapes=[
                pltpu.VMEM((256, NX * HD), BF),
                pltpu.VMEM((256, NX * HD), BF),
                pltpu.VMEM((64, HD), BF),
            ],
        ),
        compiler_params=pltpu.CompilerParams(vmem_limit_bytes=32 * 1024 * 1024),
        name="space_output",
    )(places, regrouped, embed_weight, temb, out_own, out_other)

    sent = {d: shift(share[64 * (d - 1) : 64 * d], "zh", d) for d in ORDER}
    for d in ORDER:
        base = base + sent[d].astype(F32)
    second = base.astype(BF)
    got = {d: shift(second, "zh", -d) for d in ORDER}
    second = jnp.concatenate([second] + [got[d] for d in range(1, NX)])
    got = {d: shift(second, "x", -d) for d in ORDER}
    second_all = [second] + [got[d] for d in range(1, NX)]

    weight_spec = pl.BlockSpec((3, block, HD), lambda i, s: (0, (s[0] + i) % NX, 0))
    noise = pl.pallas_call(
        time_kernel,
        out_shape=jax.ShapeDtypeStruct((256, HD), F32),
        grid_spec=pltpu.PrefetchScalarGridSpec(
            num_scalar_prefetch=1,
            grid=(NX,),
            in_specs=[whole(256, block)] * NX
            + [
                pl.BlockSpec((1, 1, block), lambda i, s: ((s[0] + i) % NX, 0, 0)),
                weight_spec,
                weight_spec,
                whole(4, HD),
                whole(256, 2 * HD),
                whole(4 * HD, HD),
            ],
            out_specs=whole(256, HD),
            scratch_shapes=[pltpu.VMEM((256, 6 * HD), F32), pltpu.VMEM((256, HD), F32)],
        ),
        compiler_params=pltpu.CompilerParams(vmem_limit_bytes=40 * 1024 * 1024),
        name="time_attention",
    )(
        places,
        *second_all,
        norm_gain[1].reshape(NX, 1, block),
        time_project,
        time_other,
        head_gain,
        att_own,
        noise_fold,
    )

    noise = lax.all_to_all(noise, ("y", "zl", "zh", "x"), split_axis=0, concat_axis=0, tiled=True)
    total = jnp.sum(noise.reshape(8, 16, 2, HD), axis=1).reshape(16, HD)

    own_first = (dot(lat_bf.reshape(16, HD), embed_weight) + temb).astype(BF)
    predicted_noise = (total + dot(own_first, noise_weight)).reshape(latents.shape)
    latents_next = (
        jnp.sqrt(alpha_next)
        * (latents - jnp.sqrt(1.0 - alpha_now) * predicted_noise)
        / jnp.sqrt(alpha_now)
        + jnp.sqrt(1.0 - alpha_next) * predicted_noise
    )
    return (predicted_noise, latents_next)


def solution(mesh):
    fine = Mesh(mesh.devices.reshape(4, 2, 4, 4, 2), ("y", "zl", "zh", "x", "c"))
    space = ("zh", "x", "c")
    rows = P(space, ("y", "zl"), None)
    placed = (
        rows,
        P(),
        P(),
        P(),
        P(),
        P(),
        P(None, None, space),
        P(space, None),
        P(None, None, space),
        P(space, None),
        P(),
    )
    return jax.shard_map(
        body,
        mesh=fine,
        in_specs=placed,
        out_specs=(rows, rows),
        check_vma=False,
    )
```

```python
import math

import jax
import jax.numpy as jnp
from jax import lax
from jax.experimental import pallas as pl
from jax.experimental.pallas import tpu as pltpu
from jax.sharding import Mesh, PartitionSpec as P

STRIDE = 20
EPS = 1e-06
NX = 4
HD = 128
ORDER = (1, 3, 2)
BF = jnp.bfloat16
F32 = jnp.float32


def shift(value, axis, step):
    size = lax.axis_size(axis)
    return lax.ppermute(value, axis, [(i, (i + step) % size) for i in range(size)])


def time_embedding(step_now, model_width):
    half_width = model_width // 2
    positions = jnp.arange(half_width, dtype=F32)
    frequency = jnp.exp(positions * (-math.log(10000.0) / half_width))
    angles = step_now.astype(F32) * frequency
    return jnp.concatenate([jnp.sin(angles), jnp.cos(angles)])


def head_norm(values, gain):
    mean_square = jnp.mean(values * values, axis=-1, keepdims=True)
    return (values * gain * lax.rsqrt(mean_square + EPS)).astype(BF)


def weigh(scores, mask=None):
    e = jnp.exp(scores * (1.0 / math.sqrt(HD)))
    if mask is not None:
        e = jnp.where(mask, e, 0.0)
    return (e / jnp.sum(e, axis=-1, keepdims=True)).astype(BF)


def dot_t(a, b):
    return lax.dot_general(a, b, (((1,), (1,)), ((), ())), preferred_element_type=F32)


def dot(a, b):
    return jnp.dot(a, b, preferred_element_type=F32)


def reorder(count, source):
    row = lax.broadcasted_iota(jnp.int32, (count, count), 0)
    col = lax.broadcasted_iota(jnp.int32, (count, count), 1)
    return (col == source(row)).astype(BF)


def fold_kernel(embed_ref, temb_ref, gain_ref, weight_ref, fold_ref, bias_ref, acc):
    step = pl.program_id(0)

    @pl.when(step == 0)
    def _():
        acc[...] = jnp.zeros_like(acc)

    gain = gain_ref[...]
    scaled = embed_ref[...].astype(F32) * gain
    high = scaled.astype(BF)
    low = (scaled - high.astype(F32)).astype(BF)
    time = temb_ref[...] * gain
    time_high = time.astype(BF).astype(F32)
    row = lax.broadcasted_iota(jnp.int32, (16, time.shape[1]), 0)
    extra = jnp.where(row == 0, time_high, jnp.where(row == 1, time - time_high, 0.0)).astype(BF)
    weights = jnp.concatenate([weight_ref[i] for i in range(3)], axis=1)
    share = dot(jnp.concatenate([high, low], axis=0), weights)
    acc[:HD, :] += share[:HD] + share[HD:]
    share = dot(extra, weights)
    acc[HD:, :] += share

    @pl.when(step == pl.num_programs(0) - 1)
    def _():
        fold = acc[:HD, :]
        fold_high = fold.astype(BF)
        fold_ref[:HD, :] = fold_high
        fold_ref[HD:, :] = (fold - fold_high.astype(F32)).astype(BF)
        bias = acc[HD : HD + 1, :] + acc[HD + 1 : HD + 2, :]
        bias_ref[...] = jnp.broadcast_to(bias, bias_ref.shape)


def space_kernel(place_ref, lat_ref, embed_ref, temb_ref, fold_ref, bias_ref, gain_ref, out_ref):
    z_here = place_ref[1]
    core = place_ref[2]

    def source(row):
        z = (z_here + (row >> 2)) & 3
        frame = (row >> 8) & 1
        return ((((((z * 4 + (row & 3)) * 2 + ((row >> 4) & 1)) << 3) + ((row >> 5) & 7)) << 1) + frame)

    lat = dot(reorder(512, source), lat_ref[...]).astype(BF)
    width = embed_ref.shape[1]
    chunk = 256
    total = jnp.zeros((lat.shape[0], 128), F32)
    for start in range(0, width, chunk):
        first = dot(lat, embed_ref[:, start : start + chunk]) + temb_ref[:, start : start + chunk]
        first = first.astype(BF).astype(F32)
        square = first * first
        for lane in range(0, chunk, 128):
            total = total + square[:, lane : lane + 128]
    mean_square = jnp.sum(total, axis=-1, keepdims=True) * (1.0 / width)
    scale = lax.rsqrt(mean_square + EPS)
    proj = (dot(jnp.concatenate([lat, lat], axis=1), fold_ref[...]) + bias_ref[0:1, :]) * scale
    query = head_norm(proj[:, :HD], gain_ref[0:1, :])
    key = head_norm(proj[:, HD : 2 * HD], gain_ref[1:2, :])
    value = proj[:, 2 * HD :].astype(BF)
    parts = []
    for frame in range(2):
        rows = slice(frame * 256, (frame + 1) * 256)
        weights = weigh(dot_t(query[rows], key[rows]))
        parts.append(dot(weights, value[rows]).astype(BF))
    parts.append(jnp.where(core == 0, lat[:256], lat[256:]))
    for tm in range(8):
        for side in range(2):
            rows = slice(tm * 32 + side * 16, tm * 32 + side * 16 + 16)
            message = jnp.concatenate([part[rows] for part in parts], axis=0)
            for x in range(NX):
                start = ((tm * NX + x) * 2 + side) * 48
                out_ref[start : start + 48, :] = message


def output_kernel(
    place_ref, att_ref, embed_ref, temb_ref, own_ref, other_ref, out_ref, base_ref, att_own_ref, lhs_own, lhs_other, lat
):
    @pl.when(pl.program_id(0) == 0)
    def _():
        x_here = place_ref[0]
        core = place_ref[2]
        swap = reorder(256, lambda row: ((row & 15) << 4) + (row >> 4))

        def part(x, side, first, count):
            starts = [((tm * NX + x) * 2 + side) * 48 + first for tm in range(8)]
            return jnp.concatenate([att_ref[start : start + count, :] for start in starts], axis=0)

        for x in range(NX):
            rows = jnp.concatenate([part(x, side, 0, 32) for side in range(2)], axis=1)
            rows = dot(swap, rows).astype(BF)
            slot = pl.multiple_of(((x - x_here) & 3) * HD, HD)
            lhs_own[:, pl.ds(slot, HD)] = jnp.where(core == 0, rows[:, :HD], rows[:, HD:])
            lhs_other[:, pl.ds(slot, HD)] = jnp.where(core == 0, rows[:, HD:], rows[:, :HD])

            @pl.when(x == x_here)
            def _(rows=rows):
                att_own_ref[...] = rows

        rows = jnp.concatenate(
            [
                att_ref[(tm * NX * 2 + side) * 48 + 32 : (tm * NX * 2 + side) * 48 + 48, :]
                for tm in range(8)
                for side in range(2)
            ],
            axis=0,
        )
        lat[...] = dot(swap[:64, :], rows).astype(BF)

    width = own_ref.shape[2]
    own = own_ref[...].reshape(NX * HD, width)
    other = other_ref[...].reshape(NX * HD, width)
    share = (dot(lhs_own[...], own) + dot(lhs_other[...], other)).astype(BF)
    out_ref[...] = share[64:, :]
    first = (dot(lat[...], embed_ref[...]) + temb_ref[...]).astype(BF)
    base_ref[...] = first.astype(F32) + share[:64, :].astype(F32)


def project_block(rows, gain_ref, own_ref, other_ref, total, add):
    rows = rows.astype(F32)
    square = rows * rows
    for lane in range(0, rows.shape[1], 128):
        total = total + square[:, lane : lane + 128]
    gained = (rows * gain_ref[0]).astype(BF)
    for index in range(3):
        pair = jnp.concatenate([own_ref[index], other_ref[index]], axis=1)
        add(index, dot(gained, pair))
    return total


def time_project_kernel(
    place_ref, a0, b0, a1, b1, a3, b3, gain_ref, own_ref, other_ref, proj_ref, total_ref
):
    step = pl.program_id(0)

    @pl.when(step == 0)
    def _():
        proj_ref[...] = jnp.zeros_like(proj_ref)
        total_ref[...] = jnp.zeros_like(total_ref)

    for k, (a, b) in enumerate(((a0, b0), (a1, b1), (a3, b3))):

        @pl.when(step == k)
        def _(a=a, b=b):
            def add(index, value):
                proj_ref[:, index * 2 * HD : (index + 1) * 2 * HD] += value

            rows = jnp.concatenate([a[...], b[...]], axis=0)
            total_ref[...] = project_block(rows, gain_ref, own_ref, other_ref, total_ref[...], add)


def time_kernel(
    place_ref, a2, b2, gain_ref, own_ref, other_ref, proj_ref, total_ref, head_gain_ref, att_ref, fold_ref, out_ref
):
    parts = {}

    def add(index, value):
        parts[index] = proj_ref[:, index * 2 * HD : (index + 1) * 2 * HD] + value

    rows = jnp.concatenate([a2[...], b2[...]], axis=0)
    total = project_block(rows, gain_ref, own_ref, other_ref, total_ref[...], add)
    z_here = place_ref[1]
    width = NX * a2.shape[1]
    mean_square = jnp.sum(total, axis=-1, keepdims=True) * (1.0 / width)
    scale = lax.rsqrt(mean_square + EPS)
    count = rows.shape[0]
    row_patch = lax.broadcasted_iota(jnp.int32, (count, count), 0) >> 4
    col_patch = lax.broadcasted_iota(jnp.int32, (count, count), 1) >> 4
    mask = row_patch == col_patch
    columns = [att_ref[...]]
    for side in range(2):
        query, key, value = [parts[index][:, side * HD : (side + 1) * HD] * scale for index in range(3)]
        query = head_norm(query, head_gain_ref[2:3, :])
        key = head_norm(key, head_gain_ref[3:4, :])
        weights = weigh(dot_t(query, key), mask)
        columns.append(dot(weights, value.astype(BF)).astype(BF))

    def source(row):
        z = (((row >> 3) & 3) - z_here) & 3
        return (z << 6) + (((row >> 1) & 3) << 4) + ((row >> 5) << 1) + (row & 1)

    both = dot(reorder(count, source), jnp.concatenate(columns, axis=1)).astype(BF)
    out_ref[...] = dot(both, fold_ref[...])


def body(
    latents,
    timestep,
    alpha_table,
    norm_gain,
    head_gain,
    embed_weight,
    space_project,
    space_output,
    time_project,
    time_output,
    noise_weight,
):
    width = embed_weight.shape[1]
    block = width // NX
    core = lax.axis_index("c")
    place = lax.axis_index("x")
    places = jnp.stack([place, lax.axis_index("zh"), core]).astype(jnp.int32)
    step_now = timestep[0]
    positions = jnp.arange(alpha_table.shape[0], dtype=jnp.int32)
    alpha_now = jnp.sum(jnp.where(positions == step_now, alpha_table, 0.0))
    alpha_next = jnp.sum(jnp.where(positions == step_now + STRIDE, alpha_table, 0.0))
    temb = time_embedding(step_now, width)[None, :]

    def in_order(own, other):
        first = jnp.where(core == 0, own, other)
        second = jnp.where(core == 0, other, own)
        return jnp.stack([first, second])

    lat_bf = latents.astype(BF)
    lat_rows = jnp.broadcast_to(lat_bf.reshape(1, 16, HD), (32, 16, HD)).reshape(512, HD)
    lat_rows = lax.all_to_all(lat_rows, ("zh", "x", "c"), split_axis=0, concat_axis=0, tiled=True)

    def whole(*shape):
        return pl.BlockSpec(shape, lambda i, s: (0,) * len(shape))

    chunk = 512
    fold, bias = pl.pallas_call(
        fold_kernel,
        out_shape=(jax.ShapeDtypeStruct((2 * HD, 3 * HD), BF), jax.ShapeDtypeStruct((8, 3 * HD), F32)),
        grid=(width // chunk,),
        in_specs=[
            pl.BlockSpec((HD, chunk), lambda i: (0, i)),
            pl.BlockSpec((1, chunk), lambda i: (0, i)),
            pl.BlockSpec((1, chunk), lambda i: (0, i)),
            pl.BlockSpec((3, chunk, HD), lambda i: (0, i, 0)),
        ],
        out_specs=[
            pl.BlockSpec((2 * HD, 3 * HD), lambda i: (0, 0)),
            pl.BlockSpec((8, 3 * HD), lambda i: (0, 0)),
        ],
        scratch_shapes=[pltpu.VMEM((HD + 16, 3 * HD), F32)],
        compiler_params=pltpu.CompilerParams(vmem_limit_bytes=16 * 1024 * 1024),
        cost_estimate=pl.CostEstimate(flops=2 * 272 * 4096 * 384, bytes_accessed=5 << 20, transcendentals=0),
        name="fold_projection",
    )(embed_weight, temb, norm_gain[0:1], space_project)

    pieces = [
        lax.dynamic_slice(space_output, (0, ((place - d) % NX) * block), (HD, block)) for d in range(NX)
    ]
    got = {d: shift(pieces[d], "x", -d) for d in ORDER}
    out_own = jnp.stack([pieces[0]] + [got[d] for d in range(1, NX)])
    lat_rows, out_own = lax.optimization_barrier((lat_rows, out_own))
    out_other = shift(out_own, "c", 1)
    time_other = shift(time_project, "c", 1)
    noise_fold = jnp.concatenate(
        [dot(space_output, noise_weight).astype(BF), dot(time_output, noise_weight).astype(BF)]
    )
    noise_other = shift(noise_fold, "c", 1)
    noise_fold = jnp.concatenate(
        [in_order(noise_fold[:HD], noise_other[:HD]).reshape(2 * HD, HD), noise_fold[HD:], noise_other[HD:]]
    )

    attended = pl.pallas_call(
        space_kernel,
        out_shape=jax.ShapeDtypeStruct((64 * 48, HD), BF),
        grid_spec=pltpu.PrefetchScalarGridSpec(
            num_scalar_prefetch=1,
            grid=(1,),
            in_specs=[
                whole(512, HD),
                whole(HD, width),
                whole(1, width),
                whole(2 * HD, 3 * HD),
                whole(8, 3 * HD),
                whole(4, HD),
            ],
            out_specs=whole(64 * 48, HD),
        ),
        compiler_params=pltpu.CompilerParams(vmem_limit_bytes=32 * 1024 * 1024),
        name="space_attention",
    )(places, lat_rows, embed_weight, temb, fold, bias, head_gain)

    attended, out_other, noise_fold = lax.optimization_barrier((attended, out_other, noise_fold))
    regrouped = lax.all_to_all(attended, ("y", "zl", "x", "c"), split_axis=0, concat_axis=0, tiled=True)

    tiles = 4
    tile = block // tiles
    share, base, att_own = pl.pallas_call(
        output_kernel,
        out_shape=(
            jax.ShapeDtypeStruct((192, block), BF),
            jax.ShapeDtypeStruct((64, block), F32),
            jax.ShapeDtypeStruct((256, 2 * HD), BF),
        ),
        grid_spec=pltpu.PrefetchScalarGridSpec(
            num_scalar_prefetch=1,
            grid=(tiles,),
            in_specs=[
                whole(64 * 48, HD),
                pl.BlockSpec((HD, tile), lambda i, s: (0, s[0] * tiles + i)),
                pl.BlockSpec((1, tile), lambda i, s: (0, s[0] * tiles + i)),
                pl.BlockSpec((NX, HD, tile), lambda i, s: (0, 0, i)),
                pl.BlockSpec((NX, HD, tile), lambda i, s: (0, 0, i)),
            ],
            out_specs=[
                pl.BlockSpec((192, tile), lambda i, s: (0, i)),
                pl.BlockSpec((64, tile), lambda i, s: (0, i)),
                whole(256, 2 * HD),
            ],
            scratch_shapes=[
                pltpu.VMEM((256, NX * HD), BF),
                pltpu.VMEM((256, NX * HD), BF),
                pltpu.VMEM((64, HD), BF),
            ],
        ),
        compiler_params=pltpu.CompilerParams(vmem_limit_bytes=32 * 1024 * 1024),
        name="space_output",
    )(places, regrouped, embed_weight, temb, out_own, out_other)

    sent = {d: shift(share[64 * (d - 1) : 64 * d], "zh", d) for d in ORDER}
    for d in ORDER:
        base = base + sent[d].astype(F32)
    second = base.astype(BF)
    got = {d: shift(second, "zh", -d) for d in ORDER}
    near = jnp.concatenate([second, got[1]])
    far = jnp.concatenate([got[2], got[3]])
    near_3 = shift(near, "x", 1)
    near_1 = shift(near, "x", -1)
    far_1 = shift(far, "x", -1)
    far_3 = shift(far, "x", 1)
    near_2 = shift(near_3, "x", 1)
    far_2 = shift(far_1, "x", -1)

    half = whole(128, block)

    def time_specs(place_of):
        weights = pl.BlockSpec((3, block, HD), lambda i, s: (0, (s[0] + place_of(i)) % NX, 0))
        return [pl.BlockSpec((1, 1, block), lambda i, s: ((s[0] + place_of(i)) % NX, 0, 0)), weights, weights]

    time_weights = (norm_gain[1].reshape(NX, 1, block), time_project, time_other)
    proj, total = pl.pallas_call(
        time_project_kernel,
        out_shape=(jax.ShapeDtypeStruct((256, 6 * HD), F32), jax.ShapeDtypeStruct((256, HD), F32)),
        grid_spec=pltpu.PrefetchScalarGridSpec(
            num_scalar_prefetch=1,
            grid=(NX - 1,),
            in_specs=[half] * 6 + time_specs(lambda i: i + i // 2),
            out_specs=[whole(256, 6 * HD), whole(256, HD)],
        ),
        compiler_params=pltpu.CompilerParams(vmem_limit_bytes=32 * 1024 * 1024),
        cost_estimate=pl.CostEstimate(flops=2 * 256 * 3072 * 768, bytes_accessed=8 << 20, transcendentals=0),
        name="time_projection",
    )(places, near, far, near_1, far_1, near_3, far_3, *time_weights)
    noise = pl.pallas_call(
        time_kernel,
        out_shape=jax.ShapeDtypeStruct((256, HD), F32),
        grid_spec=pltpu.PrefetchScalarGridSpec(
            num_scalar_prefetch=1,
            grid=(1,),
            in_specs=[half] * 2
            + time_specs(lambda i: 2)
            + [whole(256, 6 * HD), whole(256, HD), whole(4, HD), whole(256, 2 * HD), whole(4 * HD, HD)],
            out_specs=whole(256, HD),
        ),
        compiler_params=pltpu.CompilerParams(vmem_limit_bytes=32 * 1024 * 1024),
        name="time_attention",
    )(places, near_2, far_2, *time_weights, proj, total, head_gain, att_own, noise_fold)

    noise = lax.all_to_all(noise, ("y", "zl", "zh", "x"), split_axis=0, concat_axis=0, tiled=True)
    total = jnp.sum(noise.reshape(8, 16, 2, HD), axis=1).reshape(16, HD)

    own_first = (dot(lat_bf.reshape(16, HD), embed_weight) + temb).astype(BF)
    predicted_noise = (total + dot(own_first, noise_weight)).reshape(latents.shape)
    latents_next = (
        jnp.sqrt(alpha_next)
        * (latents - jnp.sqrt(1.0 - alpha_now) * predicted_noise)
        / jnp.sqrt(alpha_now)
        + jnp.sqrt(1.0 - alpha_next) * predicted_noise
    )
    return (predicted_noise, latents_next)


def solution(mesh):
    fine = Mesh(mesh.devices.reshape(4, 2, 4, 4, 2), ("y", "zl", "zh", "x", "c"))
    space = ("zh", "x", "c")
    rows = P(space, ("y", "zl"), None)
    placed = (
        rows,
        P(),
        P(),
        P(),
        P(),
        P(),
        P(None, None, space),
        P(space, None),
        P(None, None, space),
        P(space, None),
        P(),
    )
    return jax.shard_map(
        body,
        mesh=fine,
        in_specs=placed,
        out_specs=(rows, rows),
        check_vma=False,
    )
```

```python
import math

import jax
import jax.numpy as jnp
from jax import lax
from jax.experimental import pallas as pl
from jax.experimental.pallas import tpu as pltpu
from jax.sharding import Mesh, PartitionSpec as P

STRIDE = 20
EPS = 1e-06
NX = 4
HD = 128
ORDER = (1, 3, 2)
BF = jnp.bfloat16
F32 = jnp.float32


def shift(value, axis, step):
    size = lax.axis_size(axis)
    return lax.ppermute(value, axis, [(i, (i + step) % size) for i in range(size)])


def time_embedding(step_now, model_width):
    half_width = model_width // 2
    positions = jnp.arange(half_width, dtype=F32)
    frequency = jnp.exp(positions * (-math.log(10000.0) / half_width))
    angles = step_now.astype(F32) * frequency
    return jnp.concatenate([jnp.sin(angles), jnp.cos(angles)])


def head_norm(values, gain):
    mean_square = jnp.mean(values * values, axis=-1, keepdims=True)
    return (values * gain * lax.rsqrt(mean_square + EPS)).astype(BF)


def weigh(scores, mask=None):
    e = jnp.exp(scores * (1.0 / math.sqrt(HD)))
    if mask is not None:
        e = jnp.where(mask, e, 0.0)
    return (e / jnp.sum(e, axis=-1, keepdims=True)).astype(BF)


def dot_t(a, b):
    return lax.dot_general(a, b, (((1,), (1,)), ((), ())), preferred_element_type=F32)


def dot(a, b):
    return jnp.dot(a, b, preferred_element_type=F32)


def reorder(count, source):
    row = lax.broadcasted_iota(jnp.int32, (count, count), 0)
    col = lax.broadcasted_iota(jnp.int32, (count, count), 1)
    return (col == source(row)).astype(BF)


def fold_kernel(embed_ref, temb_ref, gain_ref, weight_ref, fold_ref, bias_ref, held, sems):
    width = embed_ref.shape[1]
    chunk = width // sems.shape[0]
    copies = []
    for step in range(sems.shape[0]):
        rows = pl.ds(step * chunk, chunk)
        copies.append(pltpu.make_async_copy(weight_ref.at[:, rows, :], held.at[:, rows, :], sems.at[step]))
        copies[-1].start()
    fold = jnp.zeros((HD, 3 * HD), F32)
    bias = jnp.zeros((16, 3 * HD), F32)
    row = lax.broadcasted_iota(jnp.int32, (16, chunk), 0)
    for step in range(sems.shape[0]):
        columns = slice(step * chunk, (step + 1) * chunk)
        gain = gain_ref[:, columns]
        scaled = embed_ref[:, columns].astype(F32) * gain
        high = scaled.astype(BF)
        low = (scaled - high.astype(F32)).astype(BF)
        time = temb_ref[:, columns] * gain
        time_high = time.astype(BF).astype(F32)
        extra = jnp.where(row == 0, time_high, jnp.where(row == 1, time - time_high, 0.0)).astype(BF)
        copies[step].wait()
        weights = jnp.concatenate([held[i, columns, :] for i in range(3)], axis=1)
        share = dot(jnp.concatenate([high, low, extra], axis=0), weights)
        fold = fold + (share[:HD] + share[HD : 2 * HD])
        bias = bias + share[2 * HD :]
    fold_high = fold.astype(BF)
    fold_ref[:HD, :] = fold_high
    fold_ref[HD:, :] = (fold - fold_high.astype(F32)).astype(BF)
    bias_ref[...] = jnp.broadcast_to(bias[0:1, :] + bias[1:2, :], bias_ref.shape)


def space_kernel(place_ref, lat_ref, embed_ref, temb_ref, fold_ref, bias_ref, gain_ref, out_ref):
    z_here = place_ref[1]
    core = place_ref[2]

    def source(row):
        z = (z_here + (row >> 2)) & 3
        frame = (row >> 8) & 1
        return ((((((z * 4 + (row & 3)) * 2 + ((row >> 4) & 1)) << 3) + ((row >> 5) & 7)) << 1) + frame)

    lat = dot(reorder(512, source), lat_ref[...]).astype(BF)
    width = embed_ref.shape[1]
    chunk = 256
    total = jnp.zeros((lat.shape[0], 128), F32)
    for start in range(0, width, chunk):
        first = dot(lat, embed_ref[:, start : start + chunk]) + temb_ref[:, start : start + chunk]
        first = first.astype(BF).astype(F32)
        square = first * first
        for lane in range(0, chunk, 128):
            total = total + square[:, lane : lane + 128]
    mean_square = jnp.sum(total, axis=-1, keepdims=True) * (1.0 / width)
    scale = lax.rsqrt(mean_square + EPS)
    proj = (dot(jnp.concatenate([lat, lat], axis=1), fold_ref[...]) + bias_ref[0:1, :]) * scale
    query = head_norm(proj[:, :HD], gain_ref[0:1, :])
    key = head_norm(proj[:, HD : 2 * HD], gain_ref[1:2, :])
    value = proj[:, 2 * HD :].astype(BF)
    parts = []
    for frame in range(2):
        rows = slice(frame * 256, (frame + 1) * 256)
        weights = weigh(dot_t(query[rows], key[rows]))
        parts.append(dot(weights, value[rows]).astype(BF))
    parts.append(jnp.where(core == 0, lat[:256], lat[256:]))
    for tm in range(8):
        for side in range(2):
            rows = slice(tm * 32 + side * 16, tm * 32 + side * 16 + 16)
            message = jnp.concatenate([part[rows] for part in parts[:2]], axis=0)
            extra = parts[2][rows][:8]
            for x in range(NX):
                place = (tm * NX + x) * 2 + side
                out_ref[place, :32, :] = message
                out_ref[place, 32:40, :] = extra


def output_kernel(
    place_ref, att_ref, embed_ref, temb_ref, own_ref, other_ref, out_ref, base_ref, att_own_ref, lhs_own, lhs_other
):
    x_here = place_ref[0]
    core = place_ref[2]
    swap = reorder(256, lambda row: ((row & 15) << 4) + (row >> 4))
    for x in range(NX):
        sides = [
            jnp.concatenate([att_ref[(tm * NX + x) * 2 + side, :32, :] for tm in range(8)], axis=0)
            for side in range(2)
        ]
        rows = dot(swap, jnp.concatenate(sides, axis=1)).astype(BF)
        slot = pl.multiple_of(((x - x_here) & 3) * HD, HD)
        lhs_own[:, pl.ds(slot, HD)] = jnp.where(core == 0, rows[:, :HD], rows[:, HD:])
        lhs_other[:, pl.ds(slot, HD)] = jnp.where(core == 0, rows[:, HD:], rows[:, :HD])

        @pl.when(x == x_here)
        def _(rows=rows):
            att_own_ref[...] = rows

    rows = jnp.concatenate(
        [att_ref[tm * NX * 2 + side, 32:40, :].astype(F32) for tm in range(8) for side in range(2)], axis=0
    ).astype(BF)
    pick = reorder(128, lambda row: ((row & 15) << 3) + (row >> 4))
    lat = dot(pick[:64, :], rows).astype(BF)

    tile = 256
    for start in range(0, own_ref.shape[2], tile):
        columns = slice(start, start + tile)
        own = own_ref[:, :, columns].reshape(NX * HD, tile)
        other = other_ref[:, :, columns].reshape(NX * HD, tile)
        share = (dot(lhs_own[...], own) + dot(lhs_other[...], other)).astype(BF)
        out_ref[:, columns] = share[64:, :]
        first = (dot(lat, embed_ref[:, columns]) + temb_ref[:, columns]).astype(BF)
        base_ref[:, columns] = first.astype(F32) + share[:64, :].astype(F32)


def load_kernel(place_ref, own_ref, other_ref, held_ref, sems):
    block = held_ref.shape[2]
    copies = []
    for d in range(NX):
        rows = pl.ds(pl.multiple_of(((place_ref[0] + d) & 3) * block, block), block)
        for side, ref in enumerate((own_ref, other_ref)):
            target = held_ref.at[d, pl.ds(side * 3, 3)]
            copies.append(pltpu.make_async_copy(ref.at[:, rows, :], target, sems.at[d, side]))
            copies[-1].start()
    for copy in copies:
        copy.wait()


def project_block(place_ref, d, rows, gain_ref, held_ref, total, add):
    rows = rows.astype(F32)
    square = rows * rows
    for lane in range(0, rows.shape[1], 128):
        total = total + square[:, lane : lane + 128]
    gained = (rows * gain_ref[(place_ref[0] + d) & 3]).astype(BF)
    for index in range(3):
        pair = jnp.concatenate([held_ref[d, index], held_ref[d, 3 + index]], axis=1)
        add(index, dot(gained, pair))
    return total


def time_project_kernel(place_ref, a0, b0, a1, b1, a3, b3, gain_ref, held_ref, proj_ref, total_ref):
    parts = {}

    def add(index, value):
        parts[index] = parts[index] + value if index in parts else value

    total = jnp.zeros(total_ref.shape, F32)
    for d, a, b in ((0, a0, b0), (1, a1, b1), (3, a3, b3)):
        rows = jnp.concatenate([a[...], b[...]], axis=0)
        total = project_block(place_ref, d, rows, gain_ref, held_ref, total, add)
    total_ref[...] = total
    for index in range(3):
        proj_ref[:, index * 2 * HD : (index + 1) * 2 * HD] = parts[index]


def time_kernel(
    place_ref, a2, b2, gain_ref, held_ref, proj_ref, total_ref, head_gain_ref, att_ref, fold_ref, out_ref
):
    parts = {}

    def add(index, value):
        parts[index] = proj_ref[:, index * 2 * HD : (index + 1) * 2 * HD] + value

    rows = jnp.concatenate([a2[...], b2[...]], axis=0)
    total = project_block(place_ref, 2, rows, gain_ref, held_ref, total_ref[...], add)
    z_here = place_ref[1]
    width = NX * a2.shape[1]
    mean_square = jnp.sum(total, axis=-1, keepdims=True) * (1.0 / width)
    scale = lax.rsqrt(mean_square + EPS)
    count = rows.shape[0]
    row_patch = lax.broadcasted_iota(jnp.int32, (count, count), 0) >> 4
    col_patch = lax.broadcasted_iota(jnp.int32, (count, count), 1) >> 4
    mask = row_patch == col_patch
    columns = [att_ref[...]]
    for side in range(2):
        query, key, value = [parts[index][:, side * HD : (side + 1) * HD] * scale for index in range(3)]
        query = head_norm(query, head_gain_ref[2:3, :])
        key = head_norm(key, head_gain_ref[3:4, :])
        weights = weigh(dot_t(query, key), mask)
        columns.append(dot(weights, value.astype(BF)).astype(BF))

    def source(row):
        z = (((row >> 3) & 3) - z_here) & 3
        return (z << 6) + (((row >> 1) & 3) << 4) + ((row >> 5) << 1) + (row & 1)

    both = dot(reorder(count, source), jnp.concatenate(columns, axis=1)).astype(BF)
    out_ref[...] = dot(both, fold_ref[...])


def body(
    latents,
    timestep,
    alpha_table,
    norm_gain,
    head_gain,
    embed_weight,
    space_project,
    space_output,
    time_project,
    time_output,
    noise_weight,
):
    width = embed_weight.shape[1]
    block = width // NX
    core = lax.axis_index("c")
    place = lax.axis_index("x")
    places = jnp.stack([place, lax.axis_index("zh"), core]).astype(jnp.int32)
    step_now = timestep[0]
    positions = jnp.arange(alpha_table.shape[0], dtype=jnp.int32)
    alpha_now = jnp.sum(jnp.where(positions == step_now, alpha_table, 0.0))
    alpha_next = jnp.sum(jnp.where(positions == step_now + STRIDE, alpha_table, 0.0))
    temb = time_embedding(step_now, width)[None, :]

    def in_order(own, other):
        first = jnp.where(core == 0, own, other)
        second = jnp.where(core == 0, other, own)
        return jnp.stack([first, second])

    lat_bf = latents.astype(BF)
    lat_rows = jnp.broadcast_to(lat_bf.reshape(1, 16, HD), (32, 16, HD)).reshape(512, HD)
    lat_rows = lax.all_to_all(lat_rows, ("zh", "x", "c"), split_axis=0, concat_axis=0, tiled=True)

    vmem = pl.BlockSpec(memory_space=pltpu.VMEM)
    anywhere = pl.BlockSpec(memory_space=pltpu.HBM)

    def whole(*shape):
        return pl.BlockSpec(shape, lambda i, s: (0,) * len(shape))

    fold, bias = pl.pallas_call(
        fold_kernel,
        out_shape=(jax.ShapeDtypeStruct((2 * HD, 3 * HD), BF), jax.ShapeDtypeStruct((8, 3 * HD), F32)),
        in_specs=[vmem, vmem, vmem, anywhere],
        out_specs=(vmem, vmem),
        scratch_shapes=[pltpu.VMEM((3, width, HD), BF), pltpu.SemaphoreType.DMA((8,))],
        compiler_params=pltpu.CompilerParams(vmem_limit_bytes=16 * 1024 * 1024),
        cost_estimate=pl.CostEstimate(flops=2 * 272 * 4096 * 384, bytes_accessed=1024, transcendentals=0),
        name="fold_projection",
    )(embed_weight, temb, norm_gain[0:1], space_project)

    def piece_of(weight, d):
        return lax.dynamic_slice(weight, (0, ((place - d) % NX) * block), (HD, block))

    got = {d: shift(piece_of(space_output, d), "x", -d) for d in ORDER}
    got[1], late_output = lax.optimization_barrier((got[1], space_output))
    got[0] = piece_of(late_output, 0)
    out_own = jnp.stack([got[d] for d in range(NX)])
    out_other = shift(out_own, "c", 1)
    time_other = shift(time_project, "c", 1)
    attended = pl.pallas_call(
        space_kernel,
        out_shape=jax.ShapeDtypeStruct((64, 40, HD), BF),
        grid_spec=pltpu.PrefetchScalarGridSpec(
            num_scalar_prefetch=1,
            grid=(1,),
            in_specs=[vmem] * 6,
            out_specs=vmem,
        ),
        compiler_params=pltpu.CompilerParams(vmem_limit_bytes=32 * 1024 * 1024),
        name="space_attention",
    )(places, lat_rows, embed_weight, temb, fold, bias, head_gain)

    attended, out_other, time_other = lax.optimization_barrier((attended, out_other, time_other))
    regrouped = lax.all_to_all(attended, ("y", "zl", "x", "c"), split_axis=0, concat_axis=0, tiled=True)

    regrouped, late_weight = lax.optimization_barrier((regrouped, noise_weight))
    noise_fold = jnp.concatenate(
        [dot(space_output, late_weight).astype(BF), dot(time_output, late_weight).astype(BF)]
    )
    noise_other = shift(noise_fold, "c", 1)

    share, base, att_own = pl.pallas_call(
        output_kernel,
        out_shape=(
            jax.ShapeDtypeStruct((192, block), BF),
            jax.ShapeDtypeStruct((64, block), F32),
            jax.ShapeDtypeStruct((256, 2 * HD), BF),
        ),
        grid_spec=pltpu.PrefetchScalarGridSpec(
            num_scalar_prefetch=1,
            grid=(1,),
            in_specs=[
                vmem,
                pl.BlockSpec((HD, block), lambda i, s: (0, s[0])),
                pl.BlockSpec((1, block), lambda i, s: (0, s[0])),
                vmem,
                vmem,
            ],
            out_specs=[vmem, vmem, vmem],
            scratch_shapes=[pltpu.VMEM((256, NX * HD), BF), pltpu.VMEM((256, NX * HD), BF)],
        ),
        compiler_params=pltpu.CompilerParams(vmem_limit_bytes=32 * 1024 * 1024),
        name="space_output",
    )(places, regrouped, embed_weight, temb, out_own, out_other)

    sent = {d: shift(share[64 * (d - 1) : 64 * d], "zh", d) for d in ORDER}
    for d in ORDER:
        base = base + sent[d].astype(F32)
    second = base.astype(BF)
    second, noise_other = lax.optimization_barrier((second, noise_other))
    noise_fold = jnp.concatenate(
        [in_order(noise_fold[:HD], noise_other[:HD]).reshape(2 * HD, HD), noise_fold[HD:], noise_other[HD:]]
    )
    got = {d: shift(second, "zh", -d) for d in ORDER}
    near = jnp.concatenate([second, got[1]])
    far = jnp.concatenate([got[2], got[3]])
    near_3 = shift(near, "x", 1)
    near_1 = shift(near, "x", -1)
    far_1 = shift(far, "x", -1)
    far_3 = shift(far, "x", 1)
    _, time_other = lax.optimization_barrier((near, time_other))
    held = pl.pallas_call(
        load_kernel,
        out_shape=jax.ShapeDtypeStruct((NX, 6, block, HD), BF),
        in_specs=[pl.BlockSpec(memory_space=pltpu.SMEM), anywhere, anywhere],
        out_specs=vmem,
        scratch_shapes=[pltpu.SemaphoreType.DMA((NX, 2))],
        compiler_params=pltpu.CompilerParams(vmem_limit_bytes=16 * 1024 * 1024),
        cost_estimate=pl.CostEstimate(flops=2 * 272 * 4096 * 384, bytes_accessed=1024, transcendentals=0),
        name="time_weights",
    )(places, time_project, time_other)
    near_2 = shift(near_3, "x", 1)
    far_2 = shift(far_1, "x", -1)

    smem = pl.BlockSpec(memory_space=pltpu.SMEM)
    gains = norm_gain[1].reshape(NX, 1, block)
    proj, total = pl.pallas_call(
        time_project_kernel,
        out_shape=(jax.ShapeDtypeStruct((256, 6 * HD), F32), jax.ShapeDtypeStruct((256, HD), F32)),
        in_specs=[smem] + [vmem] * 8,
        out_specs=(vmem, vmem),
        compiler_params=pltpu.CompilerParams(vmem_limit_bytes=24 * 1024 * 1024),
        cost_estimate=pl.CostEstimate(flops=2 * 256 * 3072 * 768, bytes_accessed=8 << 20, transcendentals=0),
        name="time_projection",
    )(places, near, far, near_1, far_1, near_3, far_3, gains, held)
    noise = pl.pallas_call(
        time_kernel,
        out_shape=jax.ShapeDtypeStruct((256, HD), F32),
        in_specs=[smem] + [vmem] * 9,
        out_specs=vmem,
        compiler_params=pltpu.CompilerParams(vmem_limit_bytes=24 * 1024 * 1024),
        name="time_attention",
    )(places, near_2, far_2, gains, held, proj, total, head_gain, att_own, noise_fold)

    noise = lax.all_to_all(noise, ("y", "zl", "zh", "x"), split_axis=0, concat_axis=0, tiled=True)
    total = jnp.sum(noise.reshape(8, 16, 2, HD), axis=1).reshape(16, HD)

    own_first = (dot(lat_bf.reshape(16, HD), embed_weight) + temb).astype(BF)
    predicted_noise = (total + dot(own_first, noise_weight)).reshape(latents.shape)
    latents_next = (
        jnp.sqrt(alpha_next)
        * (latents - jnp.sqrt(1.0 - alpha_now) * predicted_noise)
        / jnp.sqrt(alpha_now)
        + jnp.sqrt(1.0 - alpha_next) * predicted_noise
    )
    return (predicted_noise, latents_next)


def solution(mesh):
    fine = Mesh(mesh.devices.reshape(4, 2, 4, 4, 2), ("y", "zl", "zh", "x", "c"))
    space = ("zh", "x", "c")
    rows = P(space, ("y", "zl"), None)
    placed = (
        rows,
        P(),
        P(),
        P(),
        P(),
        P(),
        P(None, None, space),
        P(space, None),
        P(None, None, space),
        P(space, None),
        P(),
    )
    return jax.shard_map(
        body,
        mesh=fine,
        in_specs=placed,
        out_specs=(rows, rows),
        check_vma=False,
    )
```

```python
import math

import jax
import jax.numpy as jnp
from jax import lax
from jax.experimental import pallas as pl
from jax.experimental.pallas import tpu as pltpu
from jax.sharding import Mesh, PartitionSpec as P

STRIDE = 20
EPS = 1e-06
NX = 4
HD = 128
ORDER = (1, 3, 2)
BF = jnp.bfloat16
F32 = jnp.float32


def shift(value, axis, step):
    size = lax.axis_size(axis)
    return lax.ppermute(value, axis, [(i, (i + step) % size) for i in range(size)])


def time_embedding(step_now, model_width):
    half_width = model_width // 2
    positions = jnp.arange(half_width, dtype=F32)
    frequency = jnp.exp(positions * (-math.log(10000.0) / half_width))
    angles = step_now.astype(F32) * frequency
    return jnp.concatenate([jnp.sin(angles), jnp.cos(angles)])


def head_norm(values, gain):
    mean_square = jnp.mean(values * values, axis=-1, keepdims=True)
    return (values * gain * lax.rsqrt(mean_square + EPS)).astype(BF)


def weigh(scores, mask=None):
    e = jnp.exp(scores * (1.0 / math.sqrt(HD)))
    if mask is not None:
        e = jnp.where(mask, e, 0.0)
    return (e / jnp.sum(e, axis=-1, keepdims=True)).astype(BF)


def dot_t(a, b):
    return lax.dot_general(a, b, (((1,), (1,)), ((), ())), preferred_element_type=F32)


def dot(a, b):
    return jnp.dot(a, b, preferred_element_type=F32)


def reorder(count, source):
    row = lax.broadcasted_iota(jnp.int32, (count, count), 0)
    col = lax.broadcasted_iota(jnp.int32, (count, count), 1)
    return (col == source(row)).astype(BF)


def fold_kernel(embed_ref, temb_ref, gain_ref, weight_ref, fold_ref, bias_ref):
    width = embed_ref.shape[1]
    chunk = 512
    fold = jnp.zeros((HD, 3 * HD), F32)
    bias = jnp.zeros((16, 3 * HD), F32)
    row = lax.broadcasted_iota(jnp.int32, (16, chunk), 0)
    for step in range(width // chunk):
        columns = slice(step * chunk, (step + 1) * chunk)
        gain = gain_ref[:, columns]
        scaled = embed_ref[:, columns].astype(F32) * gain
        high = scaled.astype(BF)
        low = (scaled - high.astype(F32)).astype(BF)
        time = temb_ref[:, columns] * gain
        time_high = time.astype(BF).astype(F32)
        extra = jnp.where(row == 0, time_high, jnp.where(row == 1, time - time_high, 0.0)).astype(BF)
        weights = jnp.concatenate([weight_ref[i, columns, :] for i in range(3)], axis=1)
        share = dot(jnp.concatenate([high, low, extra], axis=0), weights)
        fold = fold + (share[:HD] + share[HD : 2 * HD])
        bias = bias + share[2 * HD :]
    fold_high = fold.astype(BF)
    fold_ref[:HD, :] = fold_high
    fold_ref[HD:, :] = (fold - fold_high.astype(F32)).astype(BF)
    bias_ref[...] = jnp.broadcast_to(bias[0:1, :] + bias[1:2, :], bias_ref.shape)


def space_kernel(place_ref, lat_ref, embed_ref, temb_ref, fold_ref, bias_ref, gain_ref, out_ref):
    z_here = place_ref[1]
    core = place_ref[2]

    def source(row):
        z = (z_here + (row >> 2)) & 3
        frame = (row >> 8) & 1
        return ((((((z * 4 + (row & 3)) * 2 + ((row >> 4) & 1)) << 3) + ((row >> 5) & 7)) << 1) + frame)

    lat = dot(reorder(512, source), lat_ref[...]).astype(BF)
    width = embed_ref.shape[1]
    chunk = 256
    total = jnp.zeros((lat.shape[0], 128), F32)
    for start in range(0, width, chunk):
        first = dot(lat, embed_ref[:, start : start + chunk]) + temb_ref[:, start : start + chunk]
        first = first.astype(BF).astype(F32)
        square = first * first
        for lane in range(0, chunk, 128):
            total = total + square[:, lane : lane + 128]
    mean_square = jnp.sum(total, axis=-1, keepdims=True) * (1.0 / width)
    scale = lax.rsqrt(mean_square + EPS)
    proj = (dot(jnp.concatenate([lat, lat], axis=1), fold_ref[...]) + bias_ref[0:1, :]) * scale
    query = head_norm(proj[:, :HD], gain_ref[0:1, :])
    key = head_norm(proj[:, HD : 2 * HD], gain_ref[1:2, :])
    value = proj[:, 2 * HD :].astype(BF)
    parts = []
    for frame in range(2):
        rows = slice(frame * 256, (frame + 1) * 256)
        weights = weigh(dot_t(query[rows], key[rows]))
        parts.append(dot(weights, value[rows]).astype(BF))
    parts.append(jnp.where(core == 0, lat[:256], lat[256:]))
    for tm in range(8):
        for side in range(2):
            rows = slice(tm * 32 + side * 16, tm * 32 + side * 16 + 16)
            message = jnp.concatenate([part[rows] for part in parts[:2]], axis=0)
            extra = parts[2][rows][:8]
            for x in range(NX):
                place = (tm * NX + x) * 2 + side
                out_ref[place, :32, :] = message
                out_ref[place, 32:40, :] = extra


def output_kernel(
    place_ref, att_ref, embed_ref, temb_ref, own_ref, other_ref, out_ref, base_ref, att_own_ref, lhs_own, lhs_other
):
    x_here = place_ref[0]
    core = place_ref[2]
    swap = reorder(256, lambda row: ((row & 15) << 4) + (row >> 4))
    for x in range(NX):
        sides = [
            jnp.concatenate([att_ref[(tm * NX + x) * 2 + side, :32, :] for tm in range(8)], axis=0)
            for side in range(2)
        ]
        rows = dot(swap, jnp.concatenate(sides, axis=1)).astype(BF)
        slot = pl.multiple_of(((x - x_here) & 3) * HD, HD)
        lhs_own[:, pl.ds(slot, HD)] = jnp.where(core == 0, rows[:, :HD], rows[:, HD:])
        lhs_other[:, pl.ds(slot, HD)] = jnp.where(core == 0, rows[:, HD:], rows[:, :HD])

        @pl.when(x == x_here)
        def _(rows=rows):
            att_own_ref[...] = rows

    rows = jnp.concatenate(
        [att_ref[tm * NX * 2 + side, 32:40, :].astype(F32) for tm in range(8) for side in range(2)], axis=0
    ).astype(BF)
    pick = reorder(128, lambda row: ((row & 15) << 3) + (row >> 4))
    lat = dot(pick[:64, :], rows).astype(BF)

    tile = 256
    for start in range(0, own_ref.shape[2], tile):
        columns = slice(start, start + tile)
        own = own_ref[:, :, columns].reshape(NX * HD, tile)
        other = other_ref[:, :, columns].reshape(NX * HD, tile)
        share = (dot(lhs_own[...], own) + dot(lhs_other[...], other)).astype(BF)
        out_ref[:, columns] = share[64:, :]
        first = (dot(lat, embed_ref[:, columns]) + temb_ref[:, columns]).astype(BF)
        base_ref[:, columns] = first.astype(F32) + share[:64, :].astype(F32)


def load_kernel(place_ref, own_ref, other_ref, held_ref, sems):
    block = held_ref.shape[2]
    copies = []
    for d in range(NX):
        rows = pl.ds(pl.multiple_of(((place_ref[0] + d) & 3) * block, block), block)
        for side, ref in enumerate((own_ref, other_ref)):
            target = held_ref.at[d, pl.ds(side * 3, 3)]
            copies.append(pltpu.make_async_copy(ref.at[:, rows, :], target, sems.at[d, side]))
            copies[-1].start()
    for copy in copies:
        copy.wait()


def project_block(place_ref, d, rows, gain_ref, held_ref, total, add):
    rows = rows.astype(F32)
    square = rows * rows
    for lane in range(0, rows.shape[1], 128):
        total = total + square[:, lane : lane + 128]
    gained = (rows * gain_ref[(place_ref[0] + d) & 3]).astype(BF)
    for index in range(3):
        pair = jnp.concatenate([held_ref[d, index], held_ref[d, 3 + index]], axis=1)
        add(index, dot(gained, pair))
    return total


def time_project_kernel(place_ref, a0, b0, a1, b1, a3, b3, gain_ref, held_ref, proj_ref, total_ref):
    parts = {}

    def add(index, value):
        parts[index] = parts[index] + value if index in parts else value

    total = jnp.zeros(total_ref.shape, F32)
    for d, a, b in ((0, a0, b0), (1, a1, b1), (3, a3, b3)):
        rows = jnp.concatenate([a[...], b[...]], axis=0)
        total = project_block(place_ref, d, rows, gain_ref, held_ref, total, add)
    total_ref[...] = total
    for index in range(3):
        proj_ref[:, index * 2 * HD : (index + 1) * 2 * HD] = parts[index]


def time_kernel(
    place_ref, a2, b2, gain_ref, held_ref, proj_ref, total_ref, head_gain_ref, att_ref, fold_ref, out_ref
):
    parts = {}

    def add(index, value):
        parts[index] = proj_ref[:, index * 2 * HD : (index + 1) * 2 * HD] + value

    rows = jnp.concatenate([a2[...], b2[...]], axis=0)
    total = project_block(place_ref, 2, rows, gain_ref, held_ref, total_ref[...], add)
    z_here = place_ref[1]
    width = NX * a2.shape[1]
    mean_square = jnp.sum(total, axis=-1, keepdims=True) * (1.0 / width)
    scale = lax.rsqrt(mean_square + EPS)
    count = rows.shape[0]
    row_patch = lax.broadcasted_iota(jnp.int32, (count, count), 0) >> 4
    col_patch = lax.broadcasted_iota(jnp.int32, (count, count), 1) >> 4
    mask = row_patch == col_patch
    columns = [att_ref[...]]
    for side in range(2):
        query, key, value = [parts[index][:, side * HD : (side + 1) * HD] * scale for index in range(3)]
        query = head_norm(query, head_gain_ref[2:3, :])
        key = head_norm(key, head_gain_ref[3:4, :])
        weights = weigh(dot_t(query, key), mask)
        columns.append(dot(weights, value.astype(BF)).astype(BF))

    def source(row):
        z = (((row >> 3) & 3) - z_here) & 3
        return (z << 6) + (((row >> 1) & 3) << 4) + ((row >> 5) << 1) + (row & 1)

    both = dot(reorder(count, source), jnp.concatenate(columns, axis=1)).astype(BF)
    out_ref[...] = dot(both, fold_ref[...])


def body(
    latents,
    timestep,
    alpha_table,
    norm_gain,
    head_gain,
    embed_weight,
    space_project,
    space_output,
    time_project,
    time_output,
    noise_weight,
):
    width = embed_weight.shape[1]
    block = width // NX
    core = lax.axis_index("c")
    place = lax.axis_index("x")
    places = jnp.stack([place, lax.axis_index("zh"), core]).astype(jnp.int32)
    step_now = timestep[0]
    positions = jnp.arange(alpha_table.shape[0], dtype=jnp.int32)
    alpha_now = jnp.sum(jnp.where(positions == step_now, alpha_table, 0.0))
    alpha_next = jnp.sum(jnp.where(positions == step_now + STRIDE, alpha_table, 0.0))
    temb = time_embedding(step_now, width)[None, :]

    def in_order(own, other):
        first = jnp.where(core == 0, own, other)
        second = jnp.where(core == 0, other, own)
        return jnp.stack([first, second])

    lat_bf = latents.astype(BF)
    lat_rows = jnp.broadcast_to(lat_bf.reshape(1, 16, HD), (32, 16, HD)).reshape(512, HD)
    lat_rows = lax.all_to_all(lat_rows, ("zh", "x", "c"), split_axis=0, concat_axis=0, tiled=True)

    vmem = pl.BlockSpec(memory_space=pltpu.VMEM)
    anywhere = pl.BlockSpec(memory_space=pltpu.HBM)

    def whole(*shape):
        return pl.BlockSpec(shape, lambda i, s: (0,) * len(shape))

    fold, bias = pl.pallas_call(
        fold_kernel,
        out_shape=(jax.ShapeDtypeStruct((2 * HD, 3 * HD), BF), jax.ShapeDtypeStruct((8, 3 * HD), F32)),
        in_specs=[vmem] * 4,
        out_specs=(vmem, vmem),
        compiler_params=pltpu.CompilerParams(vmem_limit_bytes=16 * 1024 * 1024),
        cost_estimate=pl.CostEstimate(flops=2 * 272 * 4096 * 384, bytes_accessed=1024, transcendentals=0),
        name="fold_projection",
    )(embed_weight, temb, norm_gain[0:1], space_project)

    def piece_of(weight, d):
        return lax.dynamic_slice(weight, (0, ((place - d) % NX) * block), (HD, block))

    got = {d: shift(piece_of(space_output, d), "x", -d) for d in ORDER}
    got[1], late_output = lax.optimization_barrier((got[1], space_output))
    got[0] = piece_of(late_output, 0)
    out_own = jnp.stack([got[d] for d in range(NX)])
    out_other = shift(out_own, "c", 1)
    time_other = shift(time_project, "c", 1)
    attended = pl.pallas_call(
        space_kernel,
        out_shape=jax.ShapeDtypeStruct((64, 40, HD), BF),
        grid_spec=pltpu.PrefetchScalarGridSpec(
            num_scalar_prefetch=1,
            grid=(1,),
            in_specs=[vmem] * 6,
            out_specs=vmem,
        ),
        compiler_params=pltpu.CompilerParams(vmem_limit_bytes=32 * 1024 * 1024),
        name="space_attention",
    )(places, lat_rows, embed_weight, temb, fold, bias, head_gain)

    attended, out_other, time_other = lax.optimization_barrier((attended, out_other, time_other))
    regrouped = lax.all_to_all(attended, ("y", "zl", "x", "c"), split_axis=0, concat_axis=0, tiled=True)


    share, base, att_own = pl.pallas_call(
        output_kernel,
        out_shape=(
            jax.ShapeDtypeStruct((192, block), BF),
            jax.ShapeDtypeStruct((64, block), F32),
            jax.ShapeDtypeStruct((256, 2 * HD), BF),
        ),
        grid_spec=pltpu.PrefetchScalarGridSpec(
            num_scalar_prefetch=1,
            grid=(1,),
            in_specs=[
                vmem,
                pl.BlockSpec((HD, block), lambda i, s: (0, s[0])),
                pl.BlockSpec((1, block), lambda i, s: (0, s[0])),
                vmem,
                vmem,
            ],
            out_specs=[vmem, vmem, vmem],
            scratch_shapes=[pltpu.VMEM((256, NX * HD), BF), pltpu.VMEM((256, NX * HD), BF)],
        ),
        compiler_params=pltpu.CompilerParams(vmem_limit_bytes=32 * 1024 * 1024),
        name="space_output",
    )(places, regrouped, embed_weight, temb, out_own, out_other)

    share, late_weight, late_latents = lax.optimization_barrier((share, noise_weight, latents))
    noise_fold = jnp.concatenate(
        [dot(space_output, late_weight).astype(BF), dot(time_output, late_weight).astype(BF)]
    )
    noise_other = shift(noise_fold, "c", 1)

    sent = {d: shift(share[64 * (d - 1) : 64 * d], "zh", d) for d in ORDER}
    for d in ORDER:
        base = base + sent[d].astype(F32)
    second = base.astype(BF)
    second, noise_other = lax.optimization_barrier((second, noise_other))
    noise_fold = jnp.concatenate(
        [in_order(noise_fold[:HD], noise_other[:HD]).reshape(2 * HD, HD), noise_fold[HD:], noise_other[HD:]]
    )
    got = {d: shift(second, "zh", -d) for d in ORDER}
    near = jnp.concatenate([second, got[1]])
    far = jnp.concatenate([got[2], got[3]])
    near_3 = shift(near, "x", 1)
    near_1 = shift(near, "x", -1)
    far_1 = shift(far, "x", -1)
    far_3 = shift(far, "x", 1)
    _, time_other = lax.optimization_barrier((near, time_other))
    held = pl.pallas_call(
        load_kernel,
        out_shape=jax.ShapeDtypeStruct((NX, 6, block, HD), BF),
        in_specs=[pl.BlockSpec(memory_space=pltpu.SMEM), anywhere, anywhere],
        out_specs=vmem,
        scratch_shapes=[pltpu.SemaphoreType.DMA((NX, 2))],
        compiler_params=pltpu.CompilerParams(vmem_limit_bytes=16 * 1024 * 1024),
        cost_estimate=pl.CostEstimate(flops=2 * 272 * 4096 * 384, bytes_accessed=1024, transcendentals=0),
        name="time_weights",
    )(places, time_project, time_other)
    near_2 = shift(near_3, "x", 1)
    far_2 = shift(far_1, "x", -1)

    smem = pl.BlockSpec(memory_space=pltpu.SMEM)
    gains = norm_gain[1].reshape(NX, 1, block)
    proj, total = pl.pallas_call(
        time_project_kernel,
        out_shape=(jax.ShapeDtypeStruct((256, 6 * HD), F32), jax.ShapeDtypeStruct((256, HD), F32)),
        in_specs=[smem] + [vmem] * 8,
        out_specs=(vmem, vmem),
        compiler_params=pltpu.CompilerParams(vmem_limit_bytes=24 * 1024 * 1024),
        cost_estimate=pl.CostEstimate(flops=2 * 256 * 3072 * 768, bytes_accessed=8 << 20, transcendentals=0),
        name="time_projection",
    )(places, near, far, near_1, far_1, near_3, far_3, gains, held)
    noise = pl.pallas_call(
        time_kernel,
        out_shape=jax.ShapeDtypeStruct((256, HD), F32),
        in_specs=[smem] + [vmem] * 9,
        out_specs=vmem,
        compiler_params=pltpu.CompilerParams(vmem_limit_bytes=24 * 1024 * 1024),
        name="time_attention",
    )(places, near_2, far_2, gains, held, proj, total, head_gain, att_own, noise_fold)

    noise = lax.all_to_all(noise, ("y", "zl", "zh", "x"), split_axis=0, concat_axis=0, tiled=True)
    total = jnp.sum(noise.reshape(8, 16, 2, HD), axis=1).reshape(16, HD)

    lat_end = late_latents.astype(BF).reshape(16, HD)
    own_first = (dot(lat_end, embed_weight) + temb).astype(BF)
    predicted_noise = (total + dot(own_first, noise_weight)).reshape(latents.shape)
    latents_next = (
        jnp.sqrt(alpha_next)
        * (latents - jnp.sqrt(1.0 - alpha_now) * predicted_noise)
        / jnp.sqrt(alpha_now)
        + jnp.sqrt(1.0 - alpha_next) * predicted_noise
    )
    return (predicted_noise, latents_next)


def solution(mesh):
    fine = Mesh(mesh.devices.reshape(4, 2, 4, 4, 2), ("y", "zl", "zh", "x", "c"))
    space = ("zh", "x", "c")
    rows = P(space, ("y", "zl"), None)
    placed = (
        rows,
        P(),
        P(),
        P(),
        P(),
        P(),
        P(None, None, space),
        P(space, None),
        P(None, None, space),
        P(space, None),
        P(),
    )
    return jax.shard_map(
        body,
        mesh=fine,
        in_specs=placed,
        out_specs=(rows, rows),
        check_vma=False,
    )
```

```python
import math

import jax
import jax.numpy as jnp
from jax import lax
from jax.experimental import pallas as pl
from jax.experimental.pallas import tpu as pltpu
from jax.sharding import Mesh, PartitionSpec as P

STRIDE = 20
EPS = 1e-06
NX = 4
HD = 128
ORDER = (1, 3, 2)
BF = jnp.bfloat16
F32 = jnp.float32


def shift(value, axis, step):
    size = lax.axis_size(axis)
    return lax.ppermute(value, axis, [(i, (i + step) % size) for i in range(size)])


def time_embedding(step_now, model_width):
    half_width = model_width // 2
    positions = jnp.arange(half_width, dtype=F32)
    frequency = jnp.exp(positions * (-math.log(10000.0) / half_width))
    angles = step_now.astype(F32) * frequency
    return jnp.concatenate([jnp.sin(angles), jnp.cos(angles)])


def head_norm(values, gain):
    mean_square = jnp.mean(values * values, axis=-1, keepdims=True)
    return (values * gain * lax.rsqrt(mean_square + EPS)).astype(BF)


def weigh(scores, mask=None):
    e = jnp.exp(scores * (1.0 / math.sqrt(HD)))
    if mask is not None:
        e = jnp.where(mask, e, 0.0)
    return (e / jnp.sum(e, axis=-1, keepdims=True)).astype(BF)


def dot_t(a, b):
    return lax.dot_general(a, b, (((1,), (1,)), ((), ())), preferred_element_type=F32)


def dot(a, b):
    return jnp.dot(a, b, preferred_element_type=F32)


def reorder(count, source):
    row = lax.broadcasted_iota(jnp.int32, (count, count), 0)
    col = lax.broadcasted_iota(jnp.int32, (count, count), 1)
    return (col == source(row)).astype(BF)


def fold_kernel(embed_ref, temb_ref, gain_ref, weight_ref, fold_ref, bias_ref):
    width = embed_ref.shape[1]
    chunk = 512
    fold = jnp.zeros((HD, 3 * HD), F32)
    bias = jnp.zeros((16, 3 * HD), F32)
    row = lax.broadcasted_iota(jnp.int32, (16, chunk), 0)
    for step in range(width // chunk):
        columns = slice(step * chunk, (step + 1) * chunk)
        gain = gain_ref[:, columns]
        scaled = embed_ref[:, columns].astype(F32) * gain
        high = scaled.astype(BF)
        low = (scaled - high.astype(F32)).astype(BF)
        time = temb_ref[:, columns] * gain
        time_high = time.astype(BF).astype(F32)
        extra = jnp.where(row == 0, time_high, jnp.where(row == 1, time - time_high, 0.0)).astype(BF)
        weights = jnp.concatenate([weight_ref[i, columns, :] for i in range(3)], axis=1)
        share = dot(jnp.concatenate([high, low, extra], axis=0), weights)
        fold = fold + (share[:HD] + share[HD : 2 * HD])
        bias = bias + share[2 * HD :]
    fold_high = fold.astype(BF)
    fold_ref[:HD, :] = fold_high
    fold_ref[HD:, :] = (fold - fold_high.astype(F32)).astype(BF)
    bias_ref[...] = jnp.broadcast_to(bias[0:1, :] + bias[1:2, :], bias_ref.shape)


def space_kernel(place_ref, lat_ref, embed_ref, temb_ref, fold_ref, bias_ref, gain_ref, out_ref):
    z_here = place_ref[1]
    core = place_ref[2]

    def source(row):
        z = (z_here + (row >> 2)) & 3
        frame = (row >> 8) & 1
        return ((((((z * 4 + (row & 3)) * 2 + ((row >> 4) & 1)) << 3) + ((row >> 5) & 7)) << 1) + frame)

    lat = dot(reorder(512, source), lat_ref[...]).astype(BF)
    width = embed_ref.shape[1]
    chunk = 256
    total = jnp.zeros((lat.shape[0], 128), F32)
    for start in range(0, width, chunk):
        first = dot(lat, embed_ref[:, start : start + chunk]) + temb_ref[:, start : start + chunk]
        first = first.astype(BF).astype(F32)
        square = first * first
        for lane in range(0, chunk, 128):
            total = total + square[:, lane : lane + 128]
    mean_square = jnp.sum(total, axis=-1, keepdims=True) * (1.0 / width)
    scale = lax.rsqrt(mean_square + EPS)
    proj = (dot(jnp.concatenate([lat, lat], axis=1), fold_ref[...]) + bias_ref[0:1, :]) * scale
    query = head_norm(proj[:, :HD], gain_ref[0:1, :])
    key = head_norm(proj[:, HD : 2 * HD], gain_ref[1:2, :])
    value = proj[:, 2 * HD :].astype(BF)
    parts = []
    for frame in range(2):
        rows = slice(frame * 256, (frame + 1) * 256)
        weights = weigh(dot_t(query[rows], key[rows]))
        parts.append(dot(weights, value[rows]).astype(BF))
    parts.append(jnp.where(core == 0, lat[:256], lat[256:]))
    for tm in range(8):
        for side in range(2):
            rows = slice(tm * 32 + side * 16, tm * 32 + side * 16 + 16)
            message = jnp.concatenate([part[rows] for part in parts[:2]], axis=0)
            extra = parts[2][rows]
            for x in range(NX):
                place = (tm * NX + x) * 2 + side
                out_ref[place, :32, :] = message
                out_ref[place, 32:48, :] = extra


def output_kernel(
    place_ref, att_ref, embed_ref, temb_ref, own_ref, other_ref, out_ref, base_ref, att_own_ref, lhs_own, lhs_other
):
    x_here = place_ref[0]
    core = place_ref[2]
    swap = reorder(256, lambda row: ((row & 15) << 4) + (row >> 4))
    for x in range(NX):
        sides = [
            jnp.concatenate([att_ref[(tm * NX + x) * 2 + side, :32, :] for tm in range(8)], axis=0)
            for side in range(2)
        ]
        rows = dot(swap, jnp.concatenate(sides, axis=1)).astype(BF)
        slot = pl.multiple_of(((x - x_here) & 3) * HD, HD)
        lhs_own[:, pl.ds(slot, HD)] = jnp.where(core == 0, rows[:, :HD], rows[:, HD:])
        lhs_other[:, pl.ds(slot, HD)] = jnp.where(core == 0, rows[:, HD:], rows[:, :HD])

        @pl.when(x == x_here)
        def _(rows=rows):
            att_own_ref[...] = rows

    rows = jnp.concatenate(
        [att_ref[tm * NX * 2 + side, 32:48, :] for tm in range(8) for side in range(2)], axis=0
    )
    lat = dot(swap[:64, :], rows).astype(BF)

    tile = 256
    for start in range(0, own_ref.shape[2], tile):
        columns = slice(start, start + tile)
        own = own_ref[:, :, columns].reshape(NX * HD, tile)
        other = other_ref[:, :, columns].reshape(NX * HD, tile)
        share = (dot(lhs_own[...], own) + dot(lhs_other[...], other)).astype(BF)
        out_ref[:, columns] = share[64:, :]
        first = (dot(lat, embed_ref[:, columns]) + temb_ref[:, columns]).astype(BF)
        base_ref[:, columns] = first.astype(F32) + share[:64, :].astype(F32)


def load_kernel(place_ref, own_ref, other_ref, held_ref, sems):
    block = held_ref.shape[2]
    copies = []
    for d in range(NX):
        rows = pl.ds(pl.multiple_of(((place_ref[0] + d) & 3) * block, block), block)
        for side, ref in enumerate((own_ref, other_ref)):
            target = held_ref.at[d, pl.ds(side * 3, 3)]
            copies.append(pltpu.make_async_copy(ref.at[:, rows, :], target, sems.at[d, side]))
            copies[-1].start()
    for copy in copies:
        copy.wait()


def project_block(place_ref, d, rows, gain_ref, held_ref, total, add):
    rows = rows.astype(F32)
    square = rows * rows
    for lane in range(0, rows.shape[1], 128):
        total = total + square[:, lane : lane + 128]
    gained = (rows * gain_ref[(place_ref[0] + d) & 3]).astype(BF)
    for index in range(3):
        pair = jnp.concatenate([held_ref[d, index], held_ref[d, 3 + index]], axis=1)
        add(index, dot(gained, pair))
    return total


def time_project_kernel(place_ref, a0, b0, a1, b1, a3, b3, gain_ref, held_ref, proj_ref, total_ref):
    parts = {}

    def add(index, value):
        parts[index] = parts[index] + value if index in parts else value

    total = jnp.zeros(total_ref.shape, F32)
    for d, a, b in ((0, a0, b0), (1, a1, b1), (3, a3, b3)):
        rows = jnp.concatenate([a[...], b[...]], axis=0)
        total = project_block(place_ref, d, rows, gain_ref, held_ref, total, add)
    total_ref[...] = total
    for index in range(3):
        proj_ref[:, index * 2 * HD : (index + 1) * 2 * HD] = parts[index]


def time_kernel(
    place_ref, a2, b2, gain_ref, held_ref, proj_ref, total_ref, head_gain_ref, att_ref, fold_ref, out_ref
):
    parts = {}

    def add(index, value):
        parts[index] = proj_ref[:, index * 2 * HD : (index + 1) * 2 * HD] + value

    rows = jnp.concatenate([a2[...], b2[...]], axis=0)
    total = project_block(place_ref, 2, rows, gain_ref, held_ref, total_ref[...], add)
    z_here = place_ref[1]
    width = NX * a2.shape[1]
    mean_square = jnp.sum(total, axis=-1, keepdims=True) * (1.0 / width)
    scale = lax.rsqrt(mean_square + EPS)
    count = rows.shape[0]
    row_patch = lax.broadcasted_iota(jnp.int32, (count, count), 0) >> 4
    col_patch = lax.broadcasted_iota(jnp.int32, (count, count), 1) >> 4
    mask = row_patch == col_patch
    columns = [att_ref[...]]
    for side in range(2):
        query, key, value = [parts[index][:, side * HD : (side + 1) * HD] * scale for index in range(3)]
        query = head_norm(query, head_gain_ref[2:3, :])
        key = head_norm(key, head_gain_ref[3:4, :])
        weights = weigh(dot_t(query, key), mask)
        columns.append(dot(weights, value.astype(BF)).astype(BF))

    def source(row):
        z = (((row >> 3) & 3) - z_here) & 3
        return (z << 6) + (((row >> 1) & 3) << 4) + ((row >> 5) << 1) + (row & 1)

    both = dot(reorder(count, source), jnp.concatenate(columns, axis=1)).astype(BF)
    out_ref[...] = dot(both, fold_ref[...])


def body(
    latents,
    timestep,
    alpha_table,
    norm_gain,
    head_gain,
    embed_weight,
    space_project,
    space_output,
    time_project,
    time_output,
    noise_weight,
):
    width = embed_weight.shape[1]
    block = width // NX
    core = lax.axis_index("c")
    place = lax.axis_index("x")
    places = jnp.stack([place, lax.axis_index("zh"), core]).astype(jnp.int32)
    step_now = timestep[0]
    positions = jnp.arange(alpha_table.shape[0], dtype=jnp.int32)
    alpha_now = jnp.sum(jnp.where(positions == step_now, alpha_table, 0.0))
    alpha_next = jnp.sum(jnp.where(positions == step_now + STRIDE, alpha_table, 0.0))
    temb = time_embedding(step_now, width)[None, :]

    def in_order(own, other):
        first = jnp.where(core == 0, own, other)
        second = jnp.where(core == 0, other, own)
        return jnp.stack([first, second])

    lat_bf = latents.astype(BF)
    lat_rows = jnp.broadcast_to(lat_bf.reshape(1, 16, HD), (32, 16, HD)).reshape(512, HD)
    lat_rows = lax.all_to_all(lat_rows, ("zh", "x", "c"), split_axis=0, concat_axis=0, tiled=True)

    vmem = pl.BlockSpec(memory_space=pltpu.VMEM)
    anywhere = pl.BlockSpec(memory_space=pltpu.HBM)

    def whole(*shape):
        return pl.BlockSpec(shape, lambda i, s: (0,) * len(shape))

    fold, bias = pl.pallas_call(
        fold_kernel,
        out_shape=(jax.ShapeDtypeStruct((2 * HD, 3 * HD), BF), jax.ShapeDtypeStruct((8, 3 * HD), F32)),
        in_specs=[vmem] * 4,
        out_specs=(vmem, vmem),
        compiler_params=pltpu.CompilerParams(vmem_limit_bytes=16 * 1024 * 1024),
        cost_estimate=pl.CostEstimate(flops=2 * 272 * 4096 * 384, bytes_accessed=1024, transcendentals=0),
        name="fold_projection",
    )(embed_weight, temb, norm_gain[0:1], space_project)

    def piece_of(weight, d):
        return lax.dynamic_slice(weight, (0, ((place - d) % NX) * block), (HD, block))

    got = {d: shift(piece_of(space_output, d), "x", -d) for d in ORDER}
    got[1], late_output = lax.optimization_barrier((got[1], space_output))
    got[0] = piece_of(late_output, 0)
    out_own = jnp.stack([got[d] for d in range(NX)])
    out_other = shift(out_own, "c", 1)
    time_other = shift(time_project, "c", 1)
    attended = pl.pallas_call(
        space_kernel,
        out_shape=jax.ShapeDtypeStruct((64, 48, HD), BF),
        grid_spec=pltpu.PrefetchScalarGridSpec(
            num_scalar_prefetch=1,
            grid=(1,),
            in_specs=[vmem] * 6,
            out_specs=vmem,
        ),
        compiler_params=pltpu.CompilerParams(vmem_limit_bytes=32 * 1024 * 1024),
        name="space_attention",
    )(places, lat_rows, embed_weight, temb, fold, bias, head_gain)

    attended, out_other, time_other = lax.optimization_barrier((attended, out_other, time_other))
    regrouped = lax.all_to_all(attended, ("y", "zl", "x", "c"), split_axis=0, concat_axis=0, tiled=True)


    share, base, att_own = pl.pallas_call(
        output_kernel,
        out_shape=(
            jax.ShapeDtypeStruct((192, block), BF),
            jax.ShapeDtypeStruct((64, block), F32),
            jax.ShapeDtypeStruct((256, 2 * HD), BF),
        ),
        grid_spec=pltpu.PrefetchScalarGridSpec(
            num_scalar_prefetch=1,
            grid=(1,),
            in_specs=[
                vmem,
                pl.BlockSpec((HD, block), lambda i, s: (0, s[0])),
                pl.BlockSpec((1, block), lambda i, s: (0, s[0])),
                vmem,
                vmem,
            ],
            out_specs=[vmem, vmem, vmem],
            scratch_shapes=[pltpu.VMEM((256, NX * HD), BF), pltpu.VMEM((256, NX * HD), BF)],
        ),
        compiler_params=pltpu.CompilerParams(vmem_limit_bytes=32 * 1024 * 1024),
        name="space_output",
    )(places, regrouped, embed_weight, temb, out_own, out_other)

    share, late_weight, late_latents = lax.optimization_barrier((share, noise_weight, latents))
    noise_fold = jnp.concatenate(
        [dot(space_output, late_weight).astype(BF), dot(time_output, late_weight).astype(BF)]
    )
    noise_other = shift(noise_fold, "c", 1)

    sent = {d: shift(share[64 * (d - 1) : 64 * d], "zh", d) for d in ORDER}
    for d in ORDER:
        base = base + sent[d].astype(F32)
    second = base.astype(BF)
    second, noise_other = lax.optimization_barrier((second, noise_other))
    noise_fold = jnp.concatenate(
        [in_order(noise_fold[:HD], noise_other[:HD]).reshape(2 * HD, HD), noise_fold[HD:], noise_other[HD:]]
    )
    got = {d: shift(second, "zh", -d) for d in ORDER}
    near = jnp.concatenate([second, got[1]])
    far = jnp.concatenate([got[2], got[3]])
    near_3 = shift(near, "x", 1)
    near_1 = shift(near, "x", -1)
    far_1 = shift(far, "x", -1)
    far_3 = shift(far, "x", 1)
    _, time_other = lax.optimization_barrier((near, time_other))
    held = pl.pallas_call(
        load_kernel,
        out_shape=jax.ShapeDtypeStruct((NX, 6, block, HD), BF),
        in_specs=[pl.BlockSpec(memory_space=pltpu.SMEM), anywhere, anywhere],
        out_specs=vmem,
        scratch_shapes=[pltpu.SemaphoreType.DMA((NX, 2))],
        compiler_params=pltpu.CompilerParams(vmem_limit_bytes=16 * 1024 * 1024),
        cost_estimate=pl.CostEstimate(flops=2 * 272 * 4096 * 384, bytes_accessed=1024, transcendentals=0),
        name="time_weights",
    )(places, time_project, time_other)
    near_2 = shift(near_3, "x", 1)
    far_2 = shift(far_1, "x", -1)

    smem = pl.BlockSpec(memory_space=pltpu.SMEM)
    gains = norm_gain[1].reshape(NX, 1, block)
    proj, total = pl.pallas_call(
        time_project_kernel,
        out_shape=(jax.ShapeDtypeStruct((256, 6 * HD), F32), jax.ShapeDtypeStruct((256, HD), F32)),
        in_specs=[smem] + [vmem] * 8,
        out_specs=(vmem, vmem),
        compiler_params=pltpu.CompilerParams(vmem_limit_bytes=24 * 1024 * 1024),
        cost_estimate=pl.CostEstimate(flops=2 * 256 * 3072 * 768, bytes_accessed=8 << 20, transcendentals=0),
        name="time_projection",
    )(places, near, far, near_1, far_1, near_3, far_3, gains, held)
    noise = pl.pallas_call(
        time_kernel,
        out_shape=jax.ShapeDtypeStruct((256, HD), F32),
        in_specs=[smem] + [vmem] * 9,
        out_specs=vmem,
        compiler_params=pltpu.CompilerParams(vmem_limit_bytes=24 * 1024 * 1024),
        name="time_attention",
    )(places, near_2, far_2, gains, held, proj, total, head_gain, att_own, noise_fold)

    noise = lax.all_to_all(noise, ("y", "zl", "zh", "x"), split_axis=0, concat_axis=0, tiled=True)
    total = jnp.sum(noise.reshape(8, 16, 2, HD), axis=1).reshape(16, HD)

    lat_end = late_latents.astype(BF).reshape(16, HD)
    own_first = (dot(lat_end, embed_weight) + temb).astype(BF)
    predicted_noise = (total + dot(own_first, noise_weight)).reshape(latents.shape)
    latents_next = (
        jnp.sqrt(alpha_next)
        * (latents - jnp.sqrt(1.0 - alpha_now) * predicted_noise)
        / jnp.sqrt(alpha_now)
        + jnp.sqrt(1.0 - alpha_next) * predicted_noise
    )
    return (predicted_noise, latents_next)


def solution(mesh):
    fine = Mesh(mesh.devices.reshape(4, 2, 4, 4, 2), ("y", "zl", "zh", "x", "c"))
    space = ("zh", "x", "c")
    rows = P(space, ("y", "zl"), None)
    placed = (
        rows,
        P(),
        P(),
        P(),
        P(),
        P(),
        P(None, None, space),
        P(space, None),
        P(None, None, space),
        P(space, None),
        P(),
    )
    return jax.shard_map(
        body,
        mesh=fine,
        in_specs=placed,
        out_specs=(rows, rows),
        check_vma=False,
    )
```

```python
import math

import jax
import jax.numpy as jnp
from jax import lax
from jax.experimental import pallas as pl
from jax.experimental.pallas import tpu as pltpu
from jax.sharding import Mesh, PartitionSpec as P

STRIDE = 20
EPS = 1e-06
NX = 4
HD = 128
ORDER = (1, 3, 2)
BF = jnp.bfloat16
F32 = jnp.float32


def shift(value, axis, step):
    size = lax.axis_size(axis)
    return lax.ppermute(value, axis, [(i, (i + step) % size) for i in range(size)])


def time_embedding(step_now, model_width):
    half_width = model_width // 2
    positions = jnp.arange(half_width, dtype=F32)
    frequency = jnp.exp(positions * (-math.log(10000.0) / half_width))
    angles = step_now.astype(F32) * frequency
    return jnp.concatenate([jnp.sin(angles), jnp.cos(angles)])


def head_norm(values, gain):
    mean_square = jnp.mean(values * values, axis=-1, keepdims=True)
    return (values * gain * lax.rsqrt(mean_square + EPS)).astype(BF)


def weigh(scores, mask=None):
    e = jnp.exp(scores * (1.0 / math.sqrt(HD)))
    if mask is not None:
        e = jnp.where(mask, e, 0.0)
    return (e / jnp.sum(e, axis=-1, keepdims=True)).astype(BF)


def dot_t(a, b):
    return lax.dot_general(a, b, (((1,), (1,)), ((), ())), preferred_element_type=F32)


def dot(a, b):
    return jnp.dot(a, b, preferred_element_type=F32)


def reorder(count, source):
    row = lax.broadcasted_iota(jnp.int32, (count, count), 0)
    col = lax.broadcasted_iota(jnp.int32, (count, count), 1)
    return (col == source(row)).astype(BF)


def fold_kernel(embed_ref, temb_ref, gain_ref, weight_ref, fold_ref, bias_ref):
    width = embed_ref.shape[1]
    chunk = 512
    fold = jnp.zeros((HD, 3 * HD), F32)
    bias = jnp.zeros((16, 3 * HD), F32)
    row = lax.broadcasted_iota(jnp.int32, (16, chunk), 0)
    for step in range(width // chunk):
        columns = slice(step * chunk, (step + 1) * chunk)
        gain = gain_ref[:, columns]
        scaled = embed_ref[:, columns].astype(F32) * gain
        high = scaled.astype(BF)
        low = (scaled - high.astype(F32)).astype(BF)
        time = temb_ref[:, columns] * gain
        time_high = time.astype(BF).astype(F32)
        extra = jnp.where(row == 0, time_high, jnp.where(row == 1, time - time_high, 0.0)).astype(BF)
        weights = jnp.concatenate([weight_ref[i, columns, :] for i in range(3)], axis=1)
        share = dot(jnp.concatenate([high, low, extra], axis=0), weights)
        fold = fold + (share[:HD] + share[HD : 2 * HD])
        bias = bias + share[2 * HD :]
    fold_high = fold.astype(BF)
    fold_ref[:HD, :] = fold_high
    fold_ref[HD:, :] = (fold - fold_high.astype(F32)).astype(BF)
    bias_ref[...] = jnp.broadcast_to(bias[0:1, :] + bias[1:2, :], bias_ref.shape)


def space_kernel(place_ref, lat_ref, embed_ref, temb_ref, fold_ref, bias_ref, gain_ref, out_ref):
    z_here = place_ref[1]
    core = place_ref[2]

    def source(row):
        z = (z_here + (row >> 2)) & 3
        frame = (row >> 8) & 1
        return ((((((z * 4 + (row & 3)) * 2 + ((row >> 4) & 1)) << 3) + ((row >> 5) & 7)) << 1) + frame)

    lat = dot(reorder(512, source), lat_ref[...]).astype(BF)
    width = embed_ref.shape[1]
    chunk = 256
    total = jnp.zeros((lat.shape[0], 128), F32)
    for start in range(0, width, chunk):
        first = dot(lat, embed_ref[:, start : start + chunk]) + temb_ref[:, start : start + chunk]
        square = first * first
        for lane in range(0, chunk, 128):
            total = total + square[:, lane : lane + 128]
    mean_square = jnp.sum(total, axis=-1, keepdims=True) * (1.0 / width)
    scale = lax.rsqrt(mean_square + EPS)
    proj = (dot(jnp.concatenate([lat, lat], axis=1), fold_ref[...]) + bias_ref[0:1, :]) * scale
    query = head_norm(proj[:, :HD], gain_ref[0:1, :])
    key = head_norm(proj[:, HD : 2 * HD], gain_ref[1:2, :])
    value = proj[:, 2 * HD :].astype(BF)
    parts = []
    for frame in range(2):
        rows = slice(frame * 256, (frame + 1) * 256)
        weights = weigh(dot_t(query[rows], key[rows]))
        parts.append(dot(weights, value[rows]).astype(BF))
    parts.append(jnp.where(core == 0, lat[:256], lat[256:]))
    for tm in range(8):
        for side in range(2):
            rows = slice(tm * 32 + side * 16, tm * 32 + side * 16 + 16)
            message = jnp.concatenate([part[rows] for part in parts[:2]], axis=0)
            extra = parts[2][rows]
            for x in range(NX):
                place = (tm * NX + x) * 2 + side
                out_ref[place, :32, :] = message
                out_ref[place, 32:48, :] = extra


def output_kernel(
    place_ref, att_ref, embed_ref, temb_ref, own_ref, other_ref, out_ref, base_ref, att_own_ref, lhs_own, lhs_other
):
    x_here = place_ref[0]
    core = place_ref[2]
    swap = reorder(256, lambda row: ((row & 15) << 4) + (row >> 4))
    for x in range(NX):
        sides = [
            jnp.concatenate([att_ref[(tm * NX + x) * 2 + side, :32, :] for tm in range(8)], axis=0)
            for side in range(2)
        ]
        rows = dot(swap, jnp.concatenate(sides, axis=1)).astype(BF)
        slot = pl.multiple_of(((x - x_here) & 3) * HD, HD)
        lhs_own[:, pl.ds(slot, HD)] = jnp.where(core == 0, rows[:, :HD], rows[:, HD:])
        lhs_other[:, pl.ds(slot, HD)] = jnp.where(core == 0, rows[:, HD:], rows[:, :HD])

        @pl.when(x == x_here)
        def _(rows=rows):
            att_own_ref[...] = rows

    rows = jnp.concatenate(
        [att_ref[tm * NX * 2 + side, 32:48, :] for tm in range(8) for side in range(2)], axis=0
    )
    lat = dot(swap[:64, :], rows).astype(BF)

    tile = 256
    for start in range(0, own_ref.shape[2], tile):
        columns = slice(start, start + tile)
        own = own_ref[:, :, columns].reshape(NX * HD, tile)
        other = other_ref[:, :, columns].reshape(NX * HD, tile)
        share = (dot(lhs_own[...], own) + dot(lhs_other[...], other)).astype(BF)
        out_ref[:, columns] = share[64:, :]
        first = (dot(lat, embed_ref[:, columns]) + temb_ref[:, columns]).astype(BF)
        base_ref[:, columns] = first.astype(F32) + share[:64, :].astype(F32)


def load_kernel(place_ref, own_ref, other_ref, held_ref, sems):
    block = held_ref.shape[2]
    copies = []
    for d in range(NX):
        rows = pl.ds(pl.multiple_of(((place_ref[0] + d) & 3) * block, block), block)
        for side, ref in enumerate((own_ref, other_ref)):
            target = held_ref.at[d, pl.ds(side * 3, 3)]
            copies.append(pltpu.make_async_copy(ref.at[:, rows, :], target, sems.at[d, side]))
            copies[-1].start()
    for copy in copies:
        copy.wait()


def project_block(place_ref, d, rows, gain_ref, held_ref, total, add):
    rows = rows.astype(F32)
    square = rows * rows
    for lane in range(0, rows.shape[1], 128):
        total = total + square[:, lane : lane + 128]
    gained = (rows * gain_ref[(place_ref[0] + d) & 3]).astype(BF)
    for index in range(3):
        pair = jnp.concatenate([held_ref[d, index], held_ref[d, 3 + index]], axis=1)
        add(index, dot(gained, pair))
    return total


def time_project_kernel(place_ref, a0, b0, a1, b1, a3, b3, gain_ref, held_ref, proj_ref, total_ref):
    parts = {}

    def add(index, value):
        parts[index] = parts[index] + value if index in parts else value

    total = jnp.zeros(total_ref.shape, F32)
    for d, a, b in ((0, a0, b0), (1, a1, b1), (3, a3, b3)):
        rows = jnp.concatenate([a[...], b[...]], axis=0)
        total = project_block(place_ref, d, rows, gain_ref, held_ref, total, add)
    total_ref[...] = total
    for index in range(3):
        proj_ref[:, index * 2 * HD : (index + 1) * 2 * HD] = parts[index]


def time_kernel(
    place_ref, a2, b2, gain_ref, held_ref, proj_ref, total_ref, head_gain_ref, att_ref, fold_ref, out_ref
):
    parts = {}

    def add(index, value):
        parts[index] = proj_ref[:, index * 2 * HD : (index + 1) * 2 * HD] + value

    rows = jnp.concatenate([a2[...], b2[...]], axis=0)
    total = project_block(place_ref, 2, rows, gain_ref, held_ref, total_ref[...], add)
    z_here = place_ref[1]
    width = NX * a2.shape[1]
    mean_square = jnp.sum(total, axis=-1, keepdims=True) * (1.0 / width)
    scale = lax.rsqrt(mean_square + EPS)
    count = rows.shape[0]
    row_patch = lax.broadcasted_iota(jnp.int32, (count, count), 0) >> 4
    col_patch = lax.broadcasted_iota(jnp.int32, (count, count), 1) >> 4
    mask = row_patch == col_patch
    columns = [att_ref[...]]
    for side in range(2):
        query, key, value = [parts[index][:, side * HD : (side + 1) * HD] * scale for index in range(3)]
        query = head_norm(query, head_gain_ref[2:3, :])
        key = head_norm(key, head_gain_ref[3:4, :])
        weights = weigh(dot_t(query, key), mask)
        columns.append(dot(weights, value.astype(BF)).astype(BF))

    def source(row):
        z = (((row >> 3) & 3) - z_here) & 3
        return (z << 6) + (((row >> 1) & 3) << 4) + ((row >> 5) << 1) + (row & 1)

    both = dot(reorder(count, source), jnp.concatenate(columns, axis=1)).astype(BF)
    out_ref[...] = dot(both, fold_ref[...])


def body(
    latents,
    timestep,
    alpha_table,
    norm_gain,
    head_gain,
    embed_weight,
    space_project,
    space_output,
    time_project,
    time_output,
    noise_weight,
):
    width = embed_weight.shape[1]
    block = width // NX
    core = lax.axis_index("c")
    place = lax.axis_index("x")
    places = jnp.stack([place, lax.axis_index("zh"), core]).astype(jnp.int32)
    step_now = timestep[0]
    positions = jnp.arange(alpha_table.shape[0], dtype=jnp.int32)
    alpha_now = jnp.sum(jnp.where(positions == step_now, alpha_table, 0.0))
    alpha_next = jnp.sum(jnp.where(positions == step_now + STRIDE, alpha_table, 0.0))
    temb = time_embedding(step_now, width)[None, :]

    def in_order(own, other):
        first = jnp.where(core == 0, own, other)
        second = jnp.where(core == 0, other, own)
        return jnp.stack([first, second])

    lat_bf = latents.astype(BF)
    lat_rows = jnp.broadcast_to(lat_bf.reshape(1, 16, HD), (32, 16, HD)).reshape(512, HD)
    lat_rows = lax.all_to_all(lat_rows, ("zh", "x", "c"), split_axis=0, concat_axis=0, tiled=True)

    vmem = pl.BlockSpec(memory_space=pltpu.VMEM)
    anywhere = pl.BlockSpec(memory_space=pltpu.HBM)

    def whole(*shape):
        return pl.BlockSpec(shape, lambda i, s: (0,) * len(shape))

    fold, bias = pl.pallas_call(
        fold_kernel,
        out_shape=(jax.ShapeDtypeStruct((2 * HD, 3 * HD), BF), jax.ShapeDtypeStruct((8, 3 * HD), F32)),
        in_specs=[vmem] * 4,
        out_specs=(vmem, vmem),
        compiler_params=pltpu.CompilerParams(vmem_limit_bytes=16 * 1024 * 1024),
        cost_estimate=pl.CostEstimate(flops=2 * 272 * 4096 * 384, bytes_accessed=1024, transcendentals=0),
        name="fold_projection",
    )(embed_weight, temb, norm_gain[0:1], space_project)

    def piece_of(weight, d):
        return lax.dynamic_slice(weight, (0, ((place - d) % NX) * block), (HD, block))

    got = {d: shift(piece_of(space_output, d), "x", -d) for d in ORDER}
    got[1], late_output = lax.optimization_barrier((got[1], space_output))
    got[0] = piece_of(late_output, 0)
    out_own = jnp.stack([got[d] for d in range(NX)])
    out_other = shift(out_own, "c", 1)
    time_other = shift(time_project, "c", 1)
    attended = pl.pallas_call(
        space_kernel,
        out_shape=jax.ShapeDtypeStruct((64, 48, HD), BF),
        grid_spec=pltpu.PrefetchScalarGridSpec(
            num_scalar_prefetch=1,
            grid=(1,),
            in_specs=[vmem] * 6,
            out_specs=vmem,
        ),
        compiler_params=pltpu.CompilerParams(vmem_limit_bytes=32 * 1024 * 1024),
        name="space_attention",
    )(places, lat_rows, embed_weight, temb, fold, bias, head_gain)

    attended, out_other, time_other = lax.optimization_barrier((attended, out_other, time_other))
    regrouped = lax.all_to_all(attended, ("y", "zl", "x", "c"), split_axis=0, concat_axis=0, tiled=True)


    share, base, att_own = pl.pallas_call(
        output_kernel,
        out_shape=(
            jax.ShapeDtypeStruct((192, block), BF),
            jax.ShapeDtypeStruct((64, block), F32),
            jax.ShapeDtypeStruct((256, 2 * HD), BF),
        ),
        grid_spec=pltpu.PrefetchScalarGridSpec(
            num_scalar_prefetch=1,
            grid=(1,),
            in_specs=[
                vmem,
                pl.BlockSpec((HD, block), lambda i, s: (0, s[0])),
                pl.BlockSpec((1, block), lambda i, s: (0, s[0])),
                vmem,
                vmem,
            ],
            out_specs=[vmem, vmem, vmem],
            scratch_shapes=[pltpu.VMEM((256, NX * HD), BF), pltpu.VMEM((256, NX * HD), BF)],
        ),
        compiler_params=pltpu.CompilerParams(vmem_limit_bytes=32 * 1024 * 1024),
        name="space_output",
    )(places, regrouped, embed_weight, temb, out_own, out_other)

    share, late_weight, late_latents = lax.optimization_barrier((share, noise_weight, latents))
    noise_fold = jnp.concatenate(
        [dot(space_output, late_weight).astype(BF), dot(time_output, late_weight).astype(BF)]
    )
    noise_other = shift(noise_fold, "c", 1)

    sent = {d: shift(share[64 * (d - 1) : 64 * d], "zh", d) for d in ORDER}
    for d in ORDER:
        base = base + sent[d].astype(F32)
    second = base.astype(BF)
    second, noise_other = lax.optimization_barrier((second, noise_other))
    noise_fold = jnp.concatenate(
        [in_order(noise_fold[:HD], noise_other[:HD]).reshape(2 * HD, HD), noise_fold[HD:], noise_other[HD:]]
    )
    got = {d: shift(second, "zh", -d) for d in ORDER}
    near = jnp.concatenate([second, got[1]])
    far = jnp.concatenate([got[2], got[3]])
    near_3 = shift(near, "x", 1)
    near_1 = shift(near, "x", -1)
    far_1 = shift(far, "x", -1)
    far_3 = shift(far, "x", 1)
    _, time_other = lax.optimization_barrier((near, time_other))
    held = pl.pallas_call(
        load_kernel,
        out_shape=jax.ShapeDtypeStruct((NX, 6, block, HD), BF),
        in_specs=[pl.BlockSpec(memory_space=pltpu.SMEM), anywhere, anywhere],
        out_specs=vmem,
        scratch_shapes=[pltpu.SemaphoreType.DMA((NX, 2))],
        compiler_params=pltpu.CompilerParams(vmem_limit_bytes=16 * 1024 * 1024),
        cost_estimate=pl.CostEstimate(flops=2 * 272 * 4096 * 384, bytes_accessed=1024, transcendentals=0),
        name="time_weights",
    )(places, time_project, time_other)
    near_2 = shift(near_3, "x", 1)
    far_2 = shift(far_1, "x", -1)

    smem = pl.BlockSpec(memory_space=pltpu.SMEM)
    gains = norm_gain[1].reshape(NX, 1, block)
    proj, total = pl.pallas_call(
        time_project_kernel,
        out_shape=(jax.ShapeDtypeStruct((256, 6 * HD), F32), jax.ShapeDtypeStruct((256, HD), F32)),
        in_specs=[smem] + [vmem] * 8,
        out_specs=(vmem, vmem),
        compiler_params=pltpu.CompilerParams(vmem_limit_bytes=24 * 1024 * 1024),
        cost_estimate=pl.CostEstimate(flops=2 * 256 * 3072 * 768, bytes_accessed=8 << 20, transcendentals=0),
        name="time_projection",
    )(places, near, far, near_1, far_1, near_3, far_3, gains, held)
    noise = pl.pallas_call(
        time_kernel,
        out_shape=jax.ShapeDtypeStruct((256, HD), F32),
        in_specs=[smem] + [vmem] * 9,
        out_specs=vmem,
        compiler_params=pltpu.CompilerParams(vmem_limit_bytes=24 * 1024 * 1024),
        name="time_attention",
    )(places, near_2, far_2, gains, held, proj, total, head_gain, att_own, noise_fold)

    noise = lax.all_to_all(noise, ("y", "zl", "zh", "x"), split_axis=0, concat_axis=0, tiled=True)
    total = jnp.sum(noise.reshape(8, 16, 2, HD), axis=1).reshape(16, HD)

    lat_end = late_latents.astype(BF).reshape(16, HD)
    own_first = (dot(lat_end, embed_weight) + temb).astype(BF)
    predicted_noise = (total + dot(own_first, noise_weight)).reshape(latents.shape)
    latents_next = (
        jnp.sqrt(alpha_next)
        * (latents - jnp.sqrt(1.0 - alpha_now) * predicted_noise)
        / jnp.sqrt(alpha_now)
        + jnp.sqrt(1.0 - alpha_next) * predicted_noise
    )
    return (predicted_noise, latents_next)


def solution(mesh):
    fine = Mesh(mesh.devices.reshape(4, 2, 4, 4, 2), ("y", "zl", "zh", "x", "c"))
    space = ("zh", "x", "c")
    rows = P(space, ("y", "zl"), None)
    placed = (
        rows,
        P(),
        P(),
        P(),
        P(),
        P(),
        P(None, None, space),
        P(space, None),
        P(None, None, space),
        P(space, None),
        P(),
    )
    return jax.shard_map(
        body,
        mesh=fine,
        in_specs=placed,
        out_specs=(rows, rows),
        check_vma=False,
    )
```
